32 devices in a mesh: groups: 2 (over y), shard: 4 (over z), width: 2 (over x), rep: 2 (over core).
Axes of the slice: x: 2, y: 2, z: 4, core: 2. Of those that a mesh axis runs over, the one named last changes fastest.
Arguments:
- source_vecs: bfloat16 [16384, 1024], P(('groups', 'shard', 'rep'), 'width'), parts along dimension 0
- target_vecs: bfloat16 [16384, 1024], P(('groups', 'shard', 'rep'), 'width'), parts along dimension 0
- fwd_owner: int32 [16384, 4], P(('groups', 'shard', 'rep')), parts along dimension 0, may hold values from 0 to 7, all different within a row; in each aligned block of 1024 rows (0 to 1023, 1024 to 2047, ...) at most 640 rows name the same one
- fwd_row: int32 [16384, 4], P(('groups', 'shard', 'rep')), parts along dimension 0, may hold values from 0 to 1023
- bwd_owner: int32 [16384, 4], P(('groups', 'shard', 'rep')), parts along dimension 0, may hold values from 0 to 7, all different within a row; in each aligned block of 1024 rows (0 to 1023, 1024 to 2047, ...) at most 640 rows name the same one
- bwd_row: int32 [16384, 4], P(('groups', 'shard', 'rep')), parts along dimension 0, may hold values from 0 to 1023
- cand_lists: int32 [8, 16], P('groups'), parts along dimension 0, may hold values from 0 to 31, as said below
Outputs:
- best_margin: float32 [16384, 16], P(('groups', 'shard', 'rep'), 'width'), parts along dimension 0
- fwd_mean: float32 [16384], P(('groups', 'shard', 'rep')), parts along dimension 0
- bwd_mean: bfloat16 [16384], P(('groups', 'shard', 'rep')), parts along dimension 0
The draws below stay inside these ranges and needn't reach their ends.
There are 2 independent parts, one for each index of `groups`. The reference program is written for one: setup_inputs(seed, part) draws one part's arguments, and reference() takes and returns one part's arrays. A program takes and returns all parts, laid end to end along the dimension named above; each array names one. Nothing has to cross between parts.
Inputs may be any that keep to these rules, and one draw needn't show every extreme that they name: fwd_owner[i, k] * 1024 + fwd_row[i, k] is a target sentence; the 4 owners of a row differ, and among the 1024 rows of one device at most 640 name one owner. bwd_owner[j, k] * 1024 + bwd_row[j, k] is a source sentence; the 4 owners of a row differ, and among the 1024 rows of one device at most 640 name one owner. `cand_lists`: each list names 16 different target blocks; block b lies on the device of index b // 4 along shard+rep, and at most 2 blocks of one list lie on one device.
All inputs are finite; a program needn't handle non-finite values.
Results may differ from the reference program's by a relative error of at most 0.0057.
Values may be sent and summed in bfloat16 or wider, within the bound.
No kernel may reach another device: no remote copies, remote signals or barrier semaphores. Data moves between devices by JAX's collectives and lax.ppermute only.
A program may use at most 128 MiB of HBM per device.

```python
import math
import jax
import jax.numpy as jnp
import numpy as np
from jax import lax

D = 1024
K = 4
CAND = 16
BLOCK = 256
ROWS = 1024
OWNERS = 8
BLOCKS_DEV = 4
TARGET_BLOCKS = 32
SRC_BLOCKS = 4
SOURCES = 8192
CAP = 640


def shaped_rows(key, noise, row_top):
    key_row, key_col = jax.random.split(key, 2)
    rows, width = noise.shape
    row_scale = jnp.exp(jax.random.uniform(key_row, (rows, 1)) * jnp.log(row_top))
    col_rise = jnp.arange(width, dtype=jnp.float32)[None, :] / width * jnp.log(3.0)
    col_scale = jnp.exp(col_rise + jax.random.uniform(key_col, (1, width)) * jnp.log(4.0))
    return (noise * row_scale * col_scale).astype(jnp.bfloat16)


def draw_source_vecs(key, part):
    key = jax.random.fold_in(key, 11)
    key_noise, key_shape = jax.random.split(key)
    noise = jax.random.normal(key_noise, (SOURCES, D))
    return shaped_rows(key_shape, noise, 10.0)


def draw_target_vecs(key, part):
    key = jax.random.fold_in(key, 23)
    key_noise, key_shape = jax.random.split(key)
    noise = jax.random.normal(key_noise, (SOURCES, D))
    return shaped_rows(key_shape, noise, 10.0)


def draw_cand_lists(key, part):
    key = jax.random.fold_in(key, 5)
    row_keys = jax.random.split(key, SRC_BLOCKS)

    def one_list(row_key):
        key_order, key_base, key_shuffle = jax.random.split(row_key, 3)
        order = jax.random.permutation(key_order, OWNERS)
        base = jax.random.randint(key_base, (OWNERS,), 0, BLOCKS_DEV)
        places = jnp.arange(CAND)
        holder = order[places % OWNERS]
        offset = (base[holder] + places // OWNERS) % BLOCKS_DEV
        listed = holder * BLOCKS_DEV + offset
        return listed[jax.random.permutation(key_shuffle, CAND)]
    return jax.vmap(one_list)(row_keys).astype(jnp.int32)


def plant(values, rng, least, high):
    spot = [jax.random.randint(jax.random.fold_in(rng, axis), (), 0, length) for axis, length in enumerate(values.shape)]
    main_axis = values.shape.index(max(values.shape))
    neighbour = spot[:main_axis] + [(spot[main_axis] + 1) % values.shape[main_axis]] + spot[main_axis + 1:]
    return values.at[tuple(spot)].set(least).at[tuple(neighbour)].set(high)


def shared_out(own_key, own, number, rows, count, top, limit, slope):
    sequence = jax.random.permutation(own_key, count)
    crowded, ordinary = portions_of(count, rows * top, limit, slope, True), portions_of(count, rows * top, limit, slope, False)
    places = jnp.arange(count)

    def named(lengths, turn):
        used = int((lengths > 0).sum())
        fixed = max(1, used // 4)
        shifted = fixed + (places - fixed + turn * (used - fixed)) % max(1, count - fixed)
        return jnp.zeros((count,), jnp.int32).at[sequence[jnp.where(places < fixed, places, shifted)]].set(jnp.asarray(lengths, jnp.int32))

    lengths = jnp.where(number % 4 == 0, named(crowded, number // 4), named(ordinary, number - number // 4 - 1))
    mixed = jax.random.permutation(jax.random.fold_in(own, 3), count)
    source_of, sink = mixed[0:count // 2 * 2:2], mixed[1:count // 2 * 2:2]
    room = jnp.minimum(lengths[source_of] - 1, limit - lengths[sink]) // 2
    room = jnp.where((source_of == sequence[0]) | (sink == sequence[0]) | (lengths[sink] == 0), 0, jnp.maximum(room, 0))
    shifted = jax.random.randint(jax.random.fold_in(own, 4), (count // 2,), 0, 1 << 20) % (room + 1)
    lengths = lengths.at[source_of].add(-shifted).at[sink].add(shifted)
    members = jnp.searchsorted(jnp.cumsum(lengths), jnp.arange(rows * top), side="right").astype(jnp.int32)
    listing = members.reshape(top, rows).T
    listing = listing[jax.random.permutation(jax.random.fold_in(own, 1), rows)]
    turn = jax.random.randint(jax.random.fold_in(own, 2), (rows, 1), 0, top)
    return jnp.take_along_axis(listing, (jnp.arange(top)[None, :] + turn) % top, axis=1)


def portions_of(count, total, limit, lean, full):
    loads = [(1 << 20) // math.isqrt(rank ** lean) + 1 for rank in range(1, count + 1)]
    largest = limit if full else min(limit, max(-(-total // count), total * loads[0] // sum(loads)))
    least = 1 if total - largest >= count - 1 else 0
    given, surplus = [largest] + [least] * (count - 1), total - largest - least * (count - 1)
    while surplus > 0:
        movable = [i for i in range(1, count) if given[i] < largest] or [i for i in range(1, count) if given[i] < limit]
        mass, left = sum([loads[i] for i in movable]), surplus
        for i in movable:
            more = min(limit - given[i], max(1, left * loads[i] // mass), surplus)
            given[i] = given[i] + more
            surplus = surplus - more
    return np.array(given)


def setup_inputs(seed: int = 0, part: int = 0) -> dict:
    arg_keys = jax.random.split(jax.random.key(seed), 8)
    part_splits = jax.random.split(jax.random.fold_in(arg_keys[7], part), 8)
    source_vecs = draw_source_vecs(jax.random.fold_in(jax.random.fold_in(arg_keys[7], part), 71), part)
    target_vecs = draw_target_vecs(jax.random.fold_in(jax.random.fold_in(arg_keys[7], part), 71), part)
    fwd_owner_keys = jax.random.split(jax.random.fold_in(part_splits[2], 1), SOURCES // ROWS)
    fwd_owner_turns = jax.random.permutation(jax.random.fold_in(part_splits[2], 3), SOURCES // ROWS)
    fwd_owner = jax.vmap(lambda own, number: shared_out(jax.random.fold_in(part_splits[2], 2), own, number, ROWS, OWNERS, K, CAP, 2))(fwd_owner_keys, fwd_owner_turns).reshape((SOURCES, K))
    fwd_row = plant(jax.random.randint(part_splits[3], (SOURCES, K), 0, ROWS), jax.random.fold_in(part_splits[3], 1), 0, ROWS - 1).astype(jnp.int32)
    bwd_owner_keys = jax.random.split(jax.random.fold_in(part_splits[4], 1), SOURCES // ROWS)
    bwd_owner_turns = jax.random.permutation(jax.random.fold_in(part_splits[4], 3), SOURCES // ROWS)
    bwd_owner = jax.vmap(lambda own, number: shared_out(jax.random.fold_in(part_splits[4], 2), own, number, ROWS, OWNERS, K, CAP, 2))(bwd_owner_keys, bwd_owner_turns).reshape((SOURCES, K))
    bwd_row = plant(jax.random.randint(part_splits[5], (SOURCES, K), 0, ROWS), jax.random.fold_in(part_splits[5], 1), 0, ROWS - 1).astype(jnp.int32)
    cand_lists = draw_cand_lists(jax.random.fold_in(jax.random.fold_in(arg_keys[7], part), 71), part)
    return dict(source_vecs=source_vecs, target_vecs=target_vecs, fwd_owner=fwd_owner, fwd_row=fwd_row, bwd_owner=bwd_owner, bwd_row=bwd_row, cand_lists=cand_lists)


EPS = 1e-05

def rms_rows(vectors):
    values = vectors.astype(jnp.float32)
    square_mean = lax.optimization_barrier(jnp.mean(values * values, axis=1))
    return (values * lax.rsqrt(square_mean + EPS)[:, None]).astype(jnp.bfloat16)

def neighbour_mean(queries, keys, owner_ids, row_ids):
    blocks = queries.shape[0] // ROWS
    index = (owner_ids * ROWS + row_ids).astype(jnp.int32)
    query_blocks = queries.reshape(blocks, ROWS, D)
    index_blocks = index.reshape(blocks, ROWS, K)

    def one_block(args):
        query_rows, picks = args
        rows = jnp.take(keys, picks.reshape(-1), axis=0).reshape(ROWS, K, D)
        dots = jnp.einsum('rkd,rd->rk', rows.astype(jnp.float32), query_rows.astype(jnp.float32))
        return lax.optimization_barrier(jnp.mean(dots / math.sqrt(D), axis=1))
    return lax.map(one_block, (query_blocks, index_blocks)).reshape(-1)

def reference(source_vecs, target_vecs, fwd_owner, fwd_row, bwd_owner, bwd_row, cand_lists):
    src_hat = rms_rows(source_vecs)
    tgt_hat = rms_rows(target_vecs)
    fwd_mean = neighbour_mean(src_hat, tgt_hat, fwd_owner, fwd_row)
    bwd_mean = neighbour_mean(tgt_hat, src_hat, bwd_owner, bwd_row).astype(jnp.bfloat16)
    block_rows = SOURCES // SRC_BLOCKS
    src_blocks = src_hat.reshape(SRC_BLOCKS, block_rows, D)
    fwd_blocks = fwd_mean.reshape(SRC_BLOCKS, block_rows)
    tgt_blocks = tgt_hat.reshape(TARGET_BLOCKS, BLOCK, D)
    bwd_blocks = bwd_mean.reshape(TARGET_BLOCKS, BLOCK)

    def one_source(args):
        source_rows, forward, listed = args
        chosen = jnp.take(tgt_blocks, listed.astype(jnp.int32), axis=0)
        backward = jnp.take(bwd_blocks, listed.astype(jnp.int32), axis=0).astype(jnp.float32)
        sims = jnp.einsum('rd,cbd->rcb', source_rows.astype(jnp.float32), chosen.astype(jnp.float32)) / math.sqrt(D)
        margin = sims - 0.5 * (forward[:, None, None] + backward[None, :, :])
        return lax.optimization_barrier(jnp.max(margin, axis=2))
    best_margin = lax.map(one_source, (src_blocks, fwd_blocks, cand_lists)).reshape(SOURCES, CAND)
    return (best_margin, fwd_mean, bwd_mean)
```

```python
import functools
import math

import jax
import jax.numpy as jnp
from jax import lax
from jax.experimental import pallas as pl
from jax.experimental.pallas import tpu as pltpu
from jax.sharding import PartitionSpec as P

D = 1024
K = 4
CAND = 16
BLOCK = 256
EPS = 1e-05
LANES = 128
TILE = 256
MIB = 1 << 20


def normalize_kernel(*refs):
    chunks, out_ref = refs[:-1], refs[-1]
    cols = chunks[0].shape[1]
    values = [ref[...].astype(jnp.float32) for ref in chunks]
    total = sum(jnp.sum(v * v, axis=1, keepdims=True) for v in values)
    scale = lax.rsqrt(total / D + EPS)
    for d, v in enumerate(values):
        out_ref[:, d * cols : (d + 1) * cols] = (v * scale).astype(jnp.bfloat16)


def normalize_rows(chunks):
    rows, cols = chunks[0].shape
    return pl.pallas_call(
        normalize_kernel,
        grid=(rows // TILE,),
        in_specs=[pl.BlockSpec((TILE, cols), lambda i: (i, 0))] * len(chunks),
        out_specs=pl.BlockSpec((TILE, cols * len(chunks)), lambda i: (i, 0)),
        out_shape=jax.ShapeDtypeStruct((rows, cols * len(chunks)), jnp.bfloat16),
        compiler_params=pltpu.CompilerParams(vmem_limit_bytes=16 * MIB),
        cost_estimate=pl.CostEstimate(
            flops=4 * rows * D, bytes_accessed=4 * rows * D, transcendentals=rows
        ),
    )(*chunks)


def dots_kernel(reps, width, pairs, sc_ref, *refs):
    fidx_ref, bidx_ref = refs[:2]
    src_refs = refs[2 : 2 + reps]
    chunk_refs = refs[2 + reps : 2 + reps + width * pairs]
    p_in, f_in, s_ref, p_ref, f_ref, tgt, picks, bsum = refs[2 + reps + width * pairs :]
    del p_in
    step = pl.program_id(0)
    rows, cols = chunk_refs[0].shape
    length = sc_ref[3]

    @pl.when(step == 0)
    def _():
        values = []
        for d in range(width):
            value = chunk_refs[d][...].astype(jnp.float32)
            for other in range(1, pairs):
                value = value + chunk_refs[other * width + d][...].astype(jnp.float32)
            values.append(value)
        total = sum(jnp.sum(v * v, axis=1, keepdims=True) for v in values)
        scale = lax.rsqrt(total / D + EPS)
        for d, v in enumerate(values):
            tgt[:, d * cols : (d + 1) * cols] = (v * scale).astype(jnp.bfloat16)
        bidx = bidx_ref[...]
        for e in range(reps):
            place = bidx - sc_ref[4 + e]
            hit = (place >= 0) & (place < length)
            place = jnp.sum(jnp.where(hit, place + 1, 0), axis=1, keepdims=True) - 1
            picks[e] = jnp.broadcast_to(place, (rows, LANES))
        bsum[...] = jnp.zeros_like(bsum)

    row_ids = lax.broadcasted_iota(jnp.int32, (rows, TILE), 0)
    lane_ids = lax.broadcasted_iota(jnp.int32, (rows, LANES), 1)
    for e in range(reps):
        dots = lax.dot_general(
            tgt[...],
            src_refs[e][...],
            (((1,), (1,)), ((), ())),
            preferred_element_type=jnp.float32,
        )
        s_ref[e] = dots
        place = fidx_ref[e] - sc_ref[0]
        hit = (place >= 0) & (place < rows)
        place = jnp.sum(jnp.where(hit, place + 1, 0), axis=0, keepdims=True) - 1
        picked = jnp.sum(jnp.where(row_ids == place, dots, 0.0), axis=0, keepdims=True)
        f_ref[e] = f_in[e] + picked
        for g in range(TILE // LANES):
            first = step * TILE + g * LANES
            hit = picks[e] - first == lane_ids
            bsum[...] += jnp.where(hit, dots[:, g * LANES : (g + 1) * LANES], 0.0)

    @pl.when(step == pl.num_programs(0) - 1)
    def _():
        p_ref[0] = jnp.sum(jnp.transpose(bsum[...]), axis=0, keepdims=True)


def dots_call(scalars, fidx, bidx, sources, chunks, bwd_parts, fwd_parts):
    reps = len(sources)
    pairs, width = len(chunks), len(chunks[0])
    length = sources[0].shape[0]
    rows, cols = chunks[0][0].shape
    n_in = 2 + reps + width * pairs
    flat = [c for pair in chunks for c in pair]
    return pl.pallas_call(
        functools.partial(dots_kernel, reps, width, pairs),
        grid_spec=pltpu.PrefetchScalarGridSpec(
            num_scalar_prefetch=1,
            grid=(length // TILE,),
            in_specs=[
                pl.BlockSpec((reps, K, TILE), lambda j, sc: (0, 0, j)),
                pl.BlockSpec((rows, K), lambda j, sc: (sc[1], 0)),
            ]
            + [pl.BlockSpec((TILE, D), lambda j, sc: (j, 0))] * reps
            + [pl.BlockSpec((rows, cols), lambda j, sc: (0, 0))] * (width * pairs)
            + [
                pl.BlockSpec((1, 1, rows), lambda j, sc: (sc[2], 0, 0)),
                pl.BlockSpec((reps, 1, TILE), lambda j, sc: (0, 0, j)),
            ],
            out_specs=[
                pl.BlockSpec((reps, rows, TILE), lambda j, sc: (0, 0, j)),
                pl.BlockSpec((1, 1, rows), lambda j, sc: (sc[2], 0, 0)),
                pl.BlockSpec((reps, 1, TILE), lambda j, sc: (0, 0, j)),
            ],
            scratch_shapes=[
                pltpu.VMEM((rows, D), jnp.bfloat16),
                pltpu.VMEM((reps, rows, LANES), jnp.int32),
                pltpu.VMEM((rows, LANES), jnp.float32),
            ],
        ),
        out_shape=[
            jax.ShapeDtypeStruct((reps, rows, length), jnp.float32),
            jax.ShapeDtypeStruct(bwd_parts.shape, jnp.float32),
            jax.ShapeDtypeStruct(fwd_parts.shape, jnp.float32),
        ],
        input_output_aliases={n_in + 1: 1, n_in + 2: 2},
        compiler_params=pltpu.CompilerParams(vmem_limit_bytes=24 * MIB),
        cost_estimate=pl.CostEstimate(
            flops=2 * reps * length * rows * D,
            bytes_accessed=reps * length * (2 * D + 4 * rows) + 2 * rows * D,
            transcendentals=rows,
        ),
    )(scalars, fidx, bidx, *sources, *flat, bwd_parts, fwd_parts)


def margin_kernel(slots, terms, reps, sc_ref, *refs):
    s_refs = refs[:slots]
    p_refs = refs[slots : slots + terms]
    f_ref, e_ref, means, halves = refs[slots + terms :]
    step = pl.program_id(0)
    rows = s_refs[0].shape[1]
    parts = rows // BLOCK

    @pl.when(step == 0)
    def _():
        total = p_refs[0][:, 0, :]
        for ref in p_refs[1:]:
            total = total + ref[:, 0, :]
        mean = (total / (K * math.sqrt(D))).astype(jnp.bfloat16).astype(jnp.float32)
        means[...] = mean
        for t in range(slots):
            row = means[pl.ds(sc_ref[2 + t], 1), :]
            halves[t] = 0.5 * jnp.transpose(jnp.broadcast_to(row, (LANES, rows)))

    for e in range(reps):
        at = lax.rem(sc_ref[0] + e, reps)
        for t in range(slots):
            for g in range(TILE // LANES):
                lanes = slice(g * LANES, (g + 1) * LANES)
                margin = s_refs[t][e, :, lanes] * (1.0 / math.sqrt(D)) - halves[t]
                for b in range(parts):
                    top = jnp.max(margin[b * BLOCK : (b + 1) * BLOCK], axis=0, keepdims=True)
                    e_ref[at, t * parts + b : t * parts + b + 1, lanes] = top
        e_ref[at, slots * parts : slots * parts + 1, :] = f_ref[e]
        start = pl.multiple_of(lax.rem(step, rows // TILE) * TILE, LANES)
        e_ref[at, slots * parts + 1 : slots * parts + 2, :] = means[
            pl.ds(sc_ref[1], 1), pl.ds(start, TILE)
        ]


def margin_call(scalars, dots, bwd_terms, fwd_parts):
    slots, terms = len(dots), len(bwd_terms)
    reps, rows, length = dots[0].shape
    lines = slots * (rows // BLOCK) + 2
    lines = -(-lines // 8) * 8
    planes = bwd_terms[0].shape[0]
    return pl.pallas_call(
        functools.partial(margin_kernel, slots, terms, reps),
        grid_spec=pltpu.PrefetchScalarGridSpec(
            num_scalar_prefetch=1,
            grid=(length // TILE,),
            in_specs=[pl.BlockSpec((reps, rows, TILE), lambda j, sc: (0, 0, j))] * slots
            + [pl.BlockSpec(bwd_terms[0].shape, lambda j, sc: (0, 0, 0))] * terms
            + [pl.BlockSpec((reps, 1, TILE), lambda j, sc: (0, 0, j))],
            out_specs=pl.BlockSpec((reps, lines, TILE), lambda j, sc: (0, 0, j)),
            scratch_shapes=[
                pltpu.VMEM((planes, rows), jnp.float32),
                pltpu.VMEM((slots, rows, LANES), jnp.float32),
            ],
        ),
        out_shape=jax.ShapeDtypeStruct((reps, lines, length), jnp.float32),
        compiler_params=pltpu.CompilerParams(vmem_limit_bytes=48 * MIB),
        cost_estimate=pl.CostEstimate(
            flops=3 * slots * reps * rows * length,
            bytes_accessed=4 * slots * reps * rows * length,
            transcendentals=0,
        ),
    )(scalars, *dots, *bwd_terms, fwd_parts)


def final_kernel(width, reps, planes, slots, parts, sc_ref, list_ref, g_ref, best_ref, fwd_ref, bwd_ref):
    shard, wide, rep = sc_ref[0], sc_ref[1], sc_ref[2]
    fwd_line = slots * parts
    fwd = g_ref[0, 0, fwd_line : fwd_line + 1, :]
    for g in range(1, width * reps):
        fwd = fwd + g_ref[g, 0, fwd_line : fwd_line + 1, :]
    fwd = fwd / (K * math.sqrt(D))
    fwd_ref[...] = fwd
    rows = parts * BLOCK
    for v in range(width):
        part = g_ref[v * reps + rep, 0, fwd_line + 1 : fwd_line + 2, 0:rows]
        bwd_ref[:, v * rows : (v + 1) * rows] = part.astype(jnp.bfloat16)
    half = 0.5 * fwd
    per_width = best_ref.shape[0]
    both = (planes - 1) // 2
    for c in range(per_width):
        block = list_ref[wide * per_width + c]
        per_dev = parts * width
        holder = block // per_dev
        local = block - holder * per_dev
        plane = holder // reps
        peer = (local // parts) * reps + holder - plane * reps
        hops = jnp.abs(shard - plane)
        near = 2 * hops - 1 + jnp.where(plane > shard, 1, 0)
        slot = jnp.where(hops == 0, 0, jnp.where(hops <= both, near, both + hops))
        line = slot * parts + local - (local // parts) * parts
        best_ref[c : c + 1, :] = g_ref[peer, 0, pl.ds(line, 1), :] - half


def final_call(scalars, own_list, gathered, width, reps, planes, slots, parts):
    lines, length = gathered.shape[2:]
    per_width = CAND // width
    return pl.pallas_call(
        functools.partial(final_kernel, width, reps, planes, slots, parts),
        grid_spec=pltpu.PrefetchScalarGridSpec(
            num_scalar_prefetch=2,
            grid=(1,),
            in_specs=[
                pl.BlockSpec((width * reps, 1, lines, length), lambda j, sc, ls: (0, sc[2], 0, 0))
            ],
            out_specs=[
                pl.BlockSpec((per_width, length), lambda j, sc, ls: (0, 0)),
                pl.BlockSpec((1, length), lambda j, sc, ls: (0, 0)),
                pl.BlockSpec((1, length), lambda j, sc, ls: (0, 0)),
            ],
        ),
        out_shape=[
            jax.ShapeDtypeStruct((per_width, length), jnp.float32),
            jax.ShapeDtypeStruct((1, length), jnp.float32),
            jax.ShapeDtypeStruct((1, length), jnp.bfloat16),
        ],
        compiler_params=pltpu.CompilerParams(vmem_limit_bytes=16 * MIB),
    )(scalars, own_list, gathered)


def on_device(source_vecs, target_vecs, fwd_owner, fwd_row, bwd_owner, bwd_row, cand_lists):
    reps = lax.axis_size("rep")
    planes = lax.axis_size("shard")
    width = lax.axis_size("width")
    shard = lax.axis_index("shard")
    wide = lax.axis_index("width")
    rep = lax.axis_index("rep")
    length = source_vecs.shape[0]
    rows = length // width
    parts = rows // BLOCK

    def part_of(values, index):
        return lax.dynamic_slice_in_dim(values, index * rows, rows, 0)

    def shift(values, axis, count, by):
        return lax.ppermute(values, axis, [((i + by) % count, i) for i in range(count)])

    own = [part_of(target_vecs, wide)]
    for d in range(1, width):
        sent = part_of(target_vecs, lax.rem(wide + width - d, width))
        own.append(shift(sent, "width", width, d))
    arrivals = {}
    for way, by in (("up", 1), ("down", -1)):
        arrivals[way, 0] = own
        for hop in range(1, planes):
            pairs = [(i, i + by) for i in range(planes) if 0 <= i + by * 1 < planes]
            pairs = [(i, j) for i, j in pairs if 0 <= j - by * hop < planes]
            arrivals[way, hop] = [
                lax.ppermute(c, "shard", pairs) for c in arrivals[way, hop - 1]
            ]
    sources = [source_vecs] + [shift(source_vecs, "width", width, d) for d in range(1, width)]
    src = [normalize_rows(sources)]
    for e in range(1, reps):
        src.append(shift(src[0], "rep", reps, e))

    fidx_own = jnp.transpose(fwd_owner * length + fwd_row)
    fidx = jnp.stack([fidx_own] + [shift(fidx_own, "rep", reps, e) for e in range(1, reps)])
    bidx = lax.all_gather(
        part_of(bwd_owner * length + bwd_row, wide), "shard", axis=0, tiled=True
    )
    bases = [(shard * reps + lax.rem(rep + e, reps)) * length for e in range(reps)]
    bwd_parts = jnp.zeros((planes + 1, 1, rows), jnp.float32)
    fwd_parts = jnp.zeros((reps, 1, length), jnp.float32)
    both = (planes - 1) // 2
    steps = [(shard, True, [own])]
    for hop in range(1, planes):
        below, above = shard - hop, shard + hop
        if hop <= both:
            steps.append((below, below >= 0, [arrivals["up", hop]]))
            steps.append((above, above < planes, [arrivals["down", hop]]))
        else:
            plane = jnp.where(below >= 0, below, above)
            valid = (below >= 0) | (above < planes)
            steps.append((plane, valid, [arrivals["up", hop], arrivals["down", hop]]))
    dots, kept = [], []
    for plane, valid, chunks in steps:
        base = (plane * reps + rep) * length + wide * rows
        place = jnp.clip(plane, 0, planes - 1)
        row = jnp.where(valid, plane, planes)
        far = -2 * planes * reps * length
        scalars = jnp.stack(
            [jnp.where(valid, base, -far), place, row, jnp.int32(length)] + bases
        ).astype(jnp.int32)
        out, bwd_parts, fwd_parts = dots_call(
            scalars, fidx, bidx, src, chunks, bwd_parts, fwd_parts
        )
        dots.append(out)
        kept.append(place)
    terms = [bwd_parts]
    if planes <= 4:
        for d in range(1, planes):
            terms.append(shift(terms[0], "shard", planes, d))
    else:
        terms = [lax.psum(terms[0], "shard")]
    scalars = jnp.stack([rep, shard] + kept).astype(jnp.int32)
    lines = margin_call(scalars, dots, terms, fwd_parts)
    gathered = lax.all_gather(lines, ("width", "rep"), axis=0, tiled=False)
    own_list = lax.dynamic_index_in_dim(cand_lists, shard, 0, keepdims=False)
    scalars = jnp.stack([shard, wide, rep]).astype(jnp.int32)
    best, fwd_mean, bwd_mean = final_call(
        scalars, own_list, gathered, width, reps, planes, len(dots), parts
    )
    return (jnp.transpose(best), fwd_mean.reshape(-1), bwd_mean.reshape(-1))


def solution(mesh):
    in_specs = (
        P(("groups", "shard", "rep"), "width"),
        P(("groups", "shard", "rep"), "width"),
        P(("groups", "shard", "rep"), None),
        P(("groups", "shard", "rep"), None),
        P(("groups", "shard", "rep"), None),
        P(("groups", "shard", "rep"), None),
        P("groups", None),
    )
    out_specs = (
        P(("groups", "shard", "rep"), "width"),
        P(("groups", "shard", "rep")),
        P(("groups", "shard", "rep")),
    )
    return jax.shard_map(
        on_device, mesh=mesh, in_specs=in_specs, out_specs=out_specs, check_vma=False
    )
```

```python
import functools
import math

import jax
import jax.numpy as jnp
from jax import lax
from jax.experimental import pallas as pl
from jax.experimental.pallas import tpu as pltpu
from jax.sharding import PartitionSpec as P

D = 1024
K = 4
CAND = 16
BLOCK = 256
EPS = 1e-05
LANES = 128
TILE = 256
MIB = 1 << 20
CODE = 256
EXTRA = 16
VMEM_LIMIT = 56 * MIB
DOTS_LIMIT = 12 * MIB


def normalize_kernel(*refs):
    chunks, out_ref = refs[:-1], refs[-1]
    cols = chunks[0].shape[1]
    values = [ref[...].astype(jnp.float32) for ref in chunks]
    total = sum(jnp.sum(v * v, axis=1, keepdims=True) for v in values)
    scale = lax.rsqrt(total / D + EPS)
    for d, v in enumerate(values):
        out_ref[:, d * cols : (d + 1) * cols] = (v * scale).astype(jnp.bfloat16)


def normalize_rows(chunks):
    rows, cols = chunks[0].shape
    return pl.pallas_call(
        normalize_kernel,
        grid=(rows // TILE,),
        in_specs=[pl.BlockSpec((TILE, cols), lambda i: (i, 0))] * len(chunks),
        out_specs=pl.BlockSpec((TILE, cols * len(chunks)), lambda i: (i, 0)),
        out_shape=jax.ShapeDtypeStruct((rows, cols * len(chunks)), jnp.bfloat16),
        compiler_params=pltpu.CompilerParams(vmem_limit_bytes=16 * MIB),
        cost_estimate=pl.CostEstimate(
            flops=rows * D, bytes_accessed=rows * D, transcendentals=rows
        ),
    )(*chunks)


def plane_at(sc_ref, planes, hop, way):
    shard = sc_ref[0]
    if way in ("own", "up"):
        plane = shard - hop
    elif way == "down":
        plane = shard + hop
    else:
        plane = jnp.where(shard >= hop, shard - hop, shard + hop)
    return plane, (plane >= 0) & (plane < planes)


def dots_kernel(reps, width, pairs, planes, hop, way, sc_ref, *refs):
    first = hop == 0
    fidx_ref, src_refs = refs[0], refs[1 : 1 + reps]
    chunk_refs = refs[1 + reps : 1 + reps + width * pairs]
    refs = refs[1 + reps + width * pairs :]
    p_in, f_in = None, None
    if not first:
        p_in, f_in, refs = refs[0], refs[1], refs[2:]
    s_ref, p_ref, f_ref, tgt, picks, bsum = refs
    rows, cols = chunk_refs[-1].shape
    length = src_refs[0].shape[0]
    groups = length // LANES
    shard, wide, rep = sc_ref[0], sc_ref[1], sc_ref[2]
    plane, valid = plane_at(sc_ref, planes, hop, way)

    values = []
    for d in range(width):
        value = chunk_refs[d][...].astype(jnp.float32)
        for other in range(1, pairs):
            value = value + chunk_refs[other * width + d][...].astype(jnp.float32)
        if d == 0:
            codes = value[rows:]
            value = value[:rows]
        values.append(value)
    total = sum(jnp.sum(v * v, axis=1, keepdims=True) for v in values)
    scale = lax.rsqrt(total / D + EPS)
    for d, v in enumerate(values):
        tgt[:, d * cols : (d + 1) * cols] = (v * scale).astype(jnp.bfloat16)

    bidx = (codes[:K] * CODE + codes[K : 2 * K]).astype(jnp.int32)
    base = (plane * reps + rep) * length + wide * rows
    base = jnp.where(valid, base, 2 * planes * reps * length)
    lane_ids = lax.broadcasted_iota(jnp.int32, (8, LANES), 1)
    row_ids = lax.broadcasted_iota(jnp.int32, (8, length), 0)
    for e in range(reps):
        place = bidx - (shard * reps + lax.rem(rep + e, reps)) * length
        hit = (place >= 0) & (place < length)
        place = jnp.sum(jnp.where(hit, place + 1, 0), axis=0, keepdims=True) - 1
        place = jnp.broadcast_to(place.astype(jnp.float32), (LANES, rows))
        picks[...] = jnp.transpose(place).astype(jnp.int32)

        s_ref[e] = lax.dot_general(
            tgt[...],
            src_refs[e][...],
            (((1,), (1,)), ((), ())),
            preferred_element_type=jnp.float32,
        )
        place = fidx_ref[e] - base
        hit = (place >= 0) & (place < rows)
        place = jnp.sum(jnp.where(hit, place + 1, 0), axis=0, keepdims=True) - 1
        away = jnp.broadcast_to(place, (8, length)) - row_ids

        def one_line(i, total):
            line = pl.ds(pl.multiple_of(i * 8, 8), 8)
            dots = s_ref[e, line, :]
            pick = picks[line, :] - lane_ids
            part = jnp.zeros((8, LANES), jnp.float32)
            for g in range(groups):
                one = dots[:, g * LANES : (g + 1) * LANES]
                part = part + jnp.where(pick == g * LANES, one, 0.0)
            if e > 0:
                part = part + bsum[line, :]
            bsum[line, :] = part
            return total + jnp.where(away == i * 8, dots, 0.0)

        total = lax.fori_loop(
            0, rows // 8, one_line, jnp.zeros((8, length), jnp.float32), unroll=4
        )
        picked = jnp.sum(total, axis=0, keepdims=True)
        f_ref[e] = picked if first else f_in[e] + picked

    if not first:
        p_ref[...] = p_in[...]
    row = jnp.where(valid, plane, planes)
    p_ref[row] = jnp.sum(jnp.transpose(bsum[...]), axis=0, keepdims=True)


def dots_call(scalars, fidx, sources, chunks, state, planes, hop, way):
    reps = len(sources)
    pairs, width = len(chunks), len(chunks[0])
    length = sources[0].shape[0]
    rows = chunks[0][-1].shape[0]
    flat = [c for pair in chunks for c in pair]
    state = [] if state is None else state
    operands = [fidx, *sources, *flat, *state]
    vmem = pl.BlockSpec(memory_space=pltpu.VMEM)
    return pl.pallas_call(
        functools.partial(dots_kernel, reps, width, pairs, planes, hop, way),
        in_specs=[pl.BlockSpec(memory_space=pltpu.SMEM)] + [vmem] * len(operands),
        out_specs=[vmem] * 3,
        scratch_shapes=[
            pltpu.VMEM((rows, D), jnp.bfloat16),
            pltpu.VMEM((rows, LANES), jnp.int32),
            pltpu.VMEM((rows, LANES), jnp.float32),
        ],
        out_shape=[
            jax.ShapeDtypeStruct((reps, rows, length), jnp.float32),
            jax.ShapeDtypeStruct((planes + 1, 1, rows), jnp.float32),
            jax.ShapeDtypeStruct((reps, 1, length), jnp.float32),
        ],
        compiler_params=pltpu.CompilerParams(vmem_limit_bytes=DOTS_LIMIT),
        cost_estimate=pl.CostEstimate(
            flops=2 * reps * length * rows * D,
            bytes_accessed=4 * reps * length * rows,
            transcendentals=rows,
        ),
    )(scalars, *operands)


def margin_kernel(places, terms, sc_ref, *refs):
    slots = len(places)
    s_refs, p_refs, refs = refs[:slots], refs[slots : slots + terms], refs[slots + terms :]
    f_ref, e_ref, means, halves = refs
    reps, rows, lanes = s_refs[0].shape
    parts = rows // BLOCK
    planes = means.shape[0] - 1
    root = math.sqrt(D)

    @pl.when(pl.program_id(0) == 0)
    def _():
        total = p_refs[0][:, 0, :]
        for ref in p_refs[1:]:
            total = total + ref[:, 0, :]
        means[...] = (total / (K * root)).astype(jnp.bfloat16).astype(jnp.float32)
        for t, (hop, way) in enumerate(places):
            plane, _ = plane_at(sc_ref, planes, hop, way)
            row = means[pl.ds(jnp.clip(plane, 0, planes - 1), 1), :]
            halves[t] = (0.5 * root) * jnp.transpose(jnp.broadcast_to(row, (LANES, rows)))

    for e in range(reps):
        at = lax.rem(sc_ref[2] + e, reps)
        for t in range(slots):
            for b in range(parts):

                def one_line(i, top):
                    line = pl.ds(pl.multiple_of(b * BLOCK + i * 8, 8), 8)
                    half = jnp.concatenate([halves[t, line, :]] * (lanes // LANES), axis=1)
                    return jnp.maximum(top, s_refs[t][e, line, :] - half)

                top = jnp.full((8, lanes), -jnp.inf, jnp.float32)
                top = lax.fori_loop(0, BLOCK // 8, one_line, top, unroll=8)
                line = t * parts + b
                e_ref[at, line : line + 1, :] = jnp.max(top, axis=0, keepdims=True) * (1 / root)
        line = slots * parts
        e_ref[at, line : line + 1, :] = f_ref[e]
        mean = means[pl.ds(sc_ref[0], 1), :]
        for start in range(0, lanes, rows):
            e_ref[at, line + 1 : line + 2, start : start + min(rows, lanes)] = mean[:, :lanes]


def margin_call(scalars, dots, bwd_terms, fwd_parts, places, whole):
    terms, slots = len(bwd_terms), len(dots)
    reps, rows, length = dots[0].shape
    lines = -(-(slots * (rows // BLOCK) + 2) // 8) * 8
    tile = length if whole else rows
    if whole:
        s_spec = p_spec = f_spec = e_spec = pl.BlockSpec(memory_space=pltpu.VMEM)
    else:
        s_spec = pl.BlockSpec((reps, rows, tile), lambda j: (0, 0, j))
        p_spec = pl.BlockSpec(bwd_terms[0].shape, lambda j: (0, 0, 0))
        f_spec = pl.BlockSpec((reps, 1, tile), lambda j: (0, 0, j))
        e_spec = pl.BlockSpec((reps, lines, tile), lambda j: (0, 0, j))
    return pl.pallas_call(
        functools.partial(margin_kernel, places, terms),
        grid=(length // tile,),
        in_specs=[pl.BlockSpec(memory_space=pltpu.SMEM)]
        + [s_spec] * slots
        + [p_spec] * terms
        + [f_spec],
        out_specs=e_spec,
        scratch_shapes=[
            pltpu.VMEM((bwd_terms[0].shape[0], rows), jnp.float32),
            pltpu.VMEM((slots, rows, LANES), jnp.float32),
        ],
        out_shape=jax.ShapeDtypeStruct((reps, lines, length), jnp.float32),
        compiler_params=pltpu.CompilerParams(
            vmem_limit_bytes=DOTS_LIMIT if whole else VMEM_LIMIT
        ),
        cost_estimate=pl.CostEstimate(
            flops=rows * D, bytes_accessed=rows * D, transcendentals=0
        ),
    )(scalars, *dots, *bwd_terms, fwd_parts)


def final_kernel(width, reps, planes, slots, parts, sc_ref, list_ref, g_ref, best_ref, fwd_ref, bwd_ref):
    shard, wide, rep = sc_ref[0], sc_ref[1], sc_ref[2]
    both = (planes - 1) // 2
    fwd_line = slots * parts
    fwd = g_ref[0, 0, fwd_line : fwd_line + 1, :]
    for g in range(1, width * reps):
        fwd = fwd + g_ref[g, 0, fwd_line : fwd_line + 1, :]
    fwd = fwd / (K * math.sqrt(D))
    fwd_ref[...] = fwd
    rows = parts * BLOCK
    for v in range(width):
        part = g_ref[v * reps + rep, 0, fwd_line + 1 : fwd_line + 2, 0:rows]
        bwd_ref[:, v * rows : (v + 1) * rows] = part.astype(jnp.bfloat16)
    half = 0.5 * fwd
    per_width = best_ref.shape[0]
    for c in range(per_width):
        block = list_ref[wide * per_width + c]
        holder = block // (parts * width)
        local = block - holder * (parts * width)
        plane = holder // reps
        peer = (local // parts) * reps + holder - plane * reps
        hops = jnp.abs(shard - plane)
        near = 2 * hops - 1 + jnp.where(plane > shard, 1, 0)
        slot = jnp.where(hops == 0, 0, jnp.where(hops <= both, near, both + hops))
        line = slot * parts + local - (local // parts) * parts
        best_ref[c : c + 1, :] = g_ref[peer, 0, pl.ds(line, 1), :] - half


def final_call(scalars, own_list, gathered, width, reps, planes, slots, parts):
    lines, length = gathered.shape[2:]
    per_width = CAND // width
    return pl.pallas_call(
        functools.partial(final_kernel, width, reps, planes, slots, parts),
        grid_spec=pltpu.PrefetchScalarGridSpec(
            num_scalar_prefetch=2,
            grid=(1,),
            in_specs=[
                pl.BlockSpec((width * reps, 1, lines, length), lambda j, sc, ls: (0, sc[2], 0, 0))
            ],
            out_specs=[
                pl.BlockSpec((per_width, length), lambda j, sc, ls: (0, 0)),
                pl.BlockSpec((1, length), lambda j, sc, ls: (0, 0)),
                pl.BlockSpec((1, length), lambda j, sc, ls: (0, 0)),
            ],
        ),
        out_shape=[
            jax.ShapeDtypeStruct((per_width, length), jnp.float32),
            jax.ShapeDtypeStruct((1, length), jnp.float32),
            jax.ShapeDtypeStruct((1, length), jnp.bfloat16),
        ],
        compiler_params=pltpu.CompilerParams(vmem_limit_bytes=16 * MIB),
    )(scalars, own_list, gathered)


def together(*values):
    return lax.optimization_barrier(values)


def on_device(source_vecs, target_vecs, fwd_owner, fwd_row, bwd_owner, bwd_row, cand_lists):
    reps = lax.axis_size("rep")
    planes = lax.axis_size("shard")
    width = lax.axis_size("width")
    shard = lax.axis_index("shard")
    wide = lax.axis_index("width")
    rep = lax.axis_index("rep")
    length = source_vecs.shape[0]
    rows = length // width
    parts = rows // BLOCK

    def part_of(values, index, axis=0):
        return lax.dynamic_slice_in_dim(values, index * rows, rows, axis)

    def shift(values, axis, count, by):
        return lax.ppermute(values, axis, [((i + by) % count, i) for i in range(count)])

    bidx = part_of(jnp.transpose(bwd_owner * length + bwd_row), wide, 1)
    codes = [bidx // CODE, lax.rem(bidx, CODE), jnp.zeros((EXTRA - 2 * K, rows), jnp.int32)]
    codes = jnp.concatenate(codes).astype(jnp.bfloat16)
    first = [jnp.concatenate([part_of(target_vecs, wide), codes])]
    rest = []
    for d in range(1, width):
        sent = part_of(target_vecs, lax.rem(wide + width - d, width))
        rest.append(shift(sent, "width", width, d))
    fidx_own = jnp.transpose(fwd_owner * length + fwd_row)

    def over_reps(values):
        return jnp.stack([values] + [shift(values, "rep", reps, e) for e in range(1, reps)])

    fidx = over_reps(fidx_own)

    def moved(chunks, hop):
        out = []
        half = len(chunks) // 2
        ways = (chunks, chunks) if hop == 1 else (chunks[:half], chunks[half:])
        for by, side in zip((1, -1), ways):
            pairs = [(i, i + by) for i in range(planes) if 0 <= i + by < planes]
            pairs = [(i, j) for i, j in pairs if 0 <= j - by * hop < planes]
            out += [lax.ppermute(c, "shard", pairs) for c in side]
        return out

    both = (planes - 1) // 2
    dots, places, state = [], [], None
    scalars = jnp.stack([shard, wide, rep]).astype(jnp.int32)

    def arrived(hop, side):
        half = len(tails[hop]) // 2
        return [heads[hop][side]] + tails[hop][side * half : side * half + half]

    def use(hop):
        nonlocal state, fidx
        if hop == 0:
            calls = [("own", [first + tails[0]])]
        elif hop <= both:
            calls = [("up", [arrived(hop, 0)]), ("down", [arrived(hop, 1)])]
        else:
            calls = [("one", [arrived(hop, 0), arrived(hop, 1)])]
        for way, chunks in calls:
            out, *state = dots_call(scalars, fidx, src, chunks, state, planes, hop, way)
            dots.append(out)
            places.append((hop, way))

    heads, tails = {0: first}, {0: rest}
    heads[1] = moved(first, 1)
    got = together(*heads[1], *rest, source_vecs)
    heads[1], tails[0], held = list(got[:2]), list(got[2:-1]), got[-1]
    sources = [held] + [shift(held, "width", width, d) for d in range(1, width)]
    src = []
    for turn in range(2, planes + 1):
        if turn >= 4:
            for hop in range(len(set(h for h, _ in places)), turn - 2):
                use(hop)
            own_again, state[0] = together(fidx_own, state[0])
            fidx = over_reps(own_again)
            late, far = tails[turn - 2], heads[turn - 1]
            got = together(*late, *far, fidx)
            tails[turn - 2], heads[turn - 1] = list(got[: len(late)]), list(got[len(late) : -1])
            fidx = got[-1]
        fresh = moved(tails[turn - 2], turn - 1)
        ahead = moved(heads[turn - 1], turn) if turn < planes else []
        if turn == 2:
            got = together(*fresh, *ahead, *sources[1:])
            sources[1:] = got[len(fresh) + len(ahead) :]
            src = [normalize_rows(sources)]
            for e in range(1, reps):
                src.append(shift(src[0], "rep", reps, e))
        else:
            got = together(*fresh, *ahead)
        tails[turn - 1] = list(got[: len(fresh)])
        heads[turn] = list(got[len(fresh) : len(fresh) + len(ahead)])
    for hop in range(len(set(h for h, _ in places)), planes):
        use(hop)

    def over_planes(values):
        if planes > 4:
            return [lax.psum(values, "shard")]
        return [values] + [shift(values, "shard", planes, d) for d in range(1, planes)]

    lines = margin_call(
        scalars, dots, over_planes(state[0]), state[1], tuple(places), planes <= 4
    )
    gathered = lax.all_gather(lines, ("width", "rep"), axis=0, tiled=False)
    own_list = lax.dynamic_index_in_dim(cand_lists, shard, 0, keepdims=False)
    best, fwd_mean, bwd_mean = final_call(
        scalars, own_list, gathered, width, reps, planes, len(dots), parts
    )
    return (jnp.transpose(best), fwd_mean.reshape(-1), bwd_mean.reshape(-1))


def solution(mesh):
    in_specs = (
        P(("groups", "shard", "rep"), "width"),
        P(("groups", "shard", "rep"), "width"),
        P(("groups", "shard", "rep"), None),
        P(("groups", "shard", "rep"), None),
        P(("groups", "shard", "rep"), None),
        P(("groups", "shard", "rep"), None),
        P("groups", None),
    )
    out_specs = (
        P(("groups", "shard", "rep"), "width"),
        P(("groups", "shard", "rep")),
        P(("groups", "shard", "rep")),
    )
    return jax.shard_map(
        on_device, mesh=mesh, in_specs=in_specs, out_specs=out_specs, check_vma=False
    )
```

```python
import functools
import math

import jax
import jax.numpy as jnp
from jax import lax
from jax.experimental import pallas as pl
from jax.experimental.pallas import tpu as pltpu
from jax.sharding import PartitionSpec as P

D = 1024
K = 4
CAND = 16
BLOCK = 256
EPS = 1e-05
LANES = 128
TILE = 256
MIB = 1 << 20
CODE = 256
EXTRA = 16
AHEAD = 1
VMEM_LIMIT = 56 * MIB
DOTS_LIMIT = 12 * MIB


def normalize_kernel(*refs):
    chunks, out_ref = refs[:-1], refs[-1]
    cols = chunks[0].shape[1]
    values = [ref[...].astype(jnp.float32) for ref in chunks]
    total = sum(jnp.sum(v * v, axis=1, keepdims=True) for v in values)
    scale = lax.rsqrt(total / D + EPS)
    for d, v in enumerate(values):
        out_ref[:, d * cols : (d + 1) * cols] = (v * scale).astype(jnp.bfloat16)


def normalize_rows(chunks):
    rows, cols = chunks[0].shape
    return pl.pallas_call(
        normalize_kernel,
        grid=(rows // TILE,),
        in_specs=[pl.BlockSpec((TILE, cols), lambda i: (i, 0))] * len(chunks),
        out_specs=pl.BlockSpec((TILE, cols * len(chunks)), lambda i: (i, 0)),
        out_shape=jax.ShapeDtypeStruct((rows, cols * len(chunks)), jnp.bfloat16),
        compiler_params=pltpu.CompilerParams(vmem_limit_bytes=16 * MIB),
        cost_estimate=pl.CostEstimate(
            flops=rows * D, bytes_accessed=rows * D, transcendentals=rows
        ),
    )(*chunks)


def plane_at(sc_ref, planes, hop, way):
    shard = sc_ref[0]
    if way in ("own", "up"):
        plane = shard - hop
    elif way == "down":
        plane = shard + hop
    else:
        plane = jnp.where(shard >= hop, shard - hop, shard + hop)
    return plane, (plane >= 0) & (plane < planes)


def dots_kernel(reps, width, pairs, planes, hop, way, sc_ref, *refs):
    first = hop == 0
    fidx_ref, src_refs = refs[0], refs[1 : 1 + reps]
    chunk_refs = refs[1 + reps : 1 + reps + width * pairs]
    refs = refs[1 + reps + width * pairs :]
    p_in, f_in = None, None
    if not first:
        p_in, f_in, refs = refs[0], refs[1], refs[2:]
    s_ref, p_ref, f_ref, tgt, picks, bsum = refs
    rows, cols = chunk_refs[0].shape
    length = src_refs[0].shape[0]
    groups = length // LANES
    shard, wide, rep = sc_ref[0], sc_ref[1], sc_ref[2]
    plane, valid = plane_at(sc_ref, planes, hop, way)

    values = []
    for d in range(width):
        value = chunk_refs[d][...].astype(jnp.float32)
        for other in range(1, pairs):
            value = value + chunk_refs[other * width + d][...].astype(jnp.float32)
        if d == 1:
            codes = value[rows:]
            value = value[:rows]
        values.append(value)
    total = sum(jnp.sum(v * v, axis=1, keepdims=True) for v in values)
    scale = lax.rsqrt(total / D + EPS)
    for d, v in enumerate(values):
        tgt[:, d * cols : (d + 1) * cols] = (v * scale).astype(jnp.bfloat16)

    bidx = (codes[:K] * CODE + codes[K : 2 * K]).astype(jnp.int32)
    base = (plane * reps + rep) * length + wide * rows
    base = jnp.where(valid, base, 2 * planes * reps * length)
    lane_ids = lax.broadcasted_iota(jnp.int32, (8, LANES), 1)
    row_ids = lax.broadcasted_iota(jnp.int32, (8, length), 0)
    for e in range(reps):
        place = bidx - (shard * reps + lax.rem(rep + e, reps)) * length
        hit = (place >= 0) & (place < length)
        place = jnp.sum(jnp.where(hit, place + 1, 0), axis=0, keepdims=True) - 1
        place = jnp.broadcast_to(place.astype(jnp.float32), (LANES, rows))
        picks[...] = jnp.transpose(place).astype(jnp.int32)

        s_ref[e] = lax.dot_general(
            tgt[...],
            src_refs[e][...],
            (((1,), (1,)), ((), ())),
            preferred_element_type=jnp.float32,
        )
        place = fidx_ref[e] - base
        hit = (place >= 0) & (place < rows)
        place = jnp.sum(jnp.where(hit, place + 1, 0), axis=0, keepdims=True) - 1
        away = jnp.broadcast_to(place, (8, length)) - row_ids

        def one_line(i, total):
            line = pl.ds(pl.multiple_of(i * 8, 8), 8)
            dots = s_ref[e, line, :]
            pick = picks[line, :] - lane_ids
            part = jnp.zeros((8, LANES), jnp.float32)
            for g in range(groups):
                one = dots[:, g * LANES : (g + 1) * LANES]
                part = part + jnp.where(pick == g * LANES, one, 0.0)
            if e > 0:
                part = part + bsum[line, :]
            bsum[line, :] = part
            return total + jnp.where(away == i * 8, dots, 0.0)

        total = lax.fori_loop(
            0, rows // 8, one_line, jnp.zeros((8, length), jnp.float32), unroll=4
        )
        picked = jnp.sum(total, axis=0, keepdims=True)
        f_ref[e] = picked if first else f_in[e] + picked

    if not first:
        p_ref[...] = p_in[...]
    row = jnp.where(valid, plane, planes)
    p_ref[row] = jnp.sum(jnp.transpose(bsum[...]), axis=0, keepdims=True)


def dots_call(scalars, fidx, sources, chunks, state, planes, hop, way):
    reps = len(sources)
    pairs, width = len(chunks), len(chunks[0])
    length = sources[0].shape[0]
    rows = chunks[0][0].shape[0]
    flat = [c for pair in chunks for c in pair]
    state = [] if state is None else state
    operands = [fidx, *sources, *flat, *state]
    vmem = pl.BlockSpec(memory_space=pltpu.VMEM)
    return pl.pallas_call(
        functools.partial(dots_kernel, reps, width, pairs, planes, hop, way),
        in_specs=[pl.BlockSpec(memory_space=pltpu.SMEM)] + [vmem] * len(operands),
        out_specs=[vmem] * 3,
        scratch_shapes=[
            pltpu.VMEM((rows, D), jnp.bfloat16),
            pltpu.VMEM((rows, LANES), jnp.int32),
            pltpu.VMEM((rows, LANES), jnp.float32),
        ],
        out_shape=[
            jax.ShapeDtypeStruct((reps, rows, length), jnp.float32),
            jax.ShapeDtypeStruct((planes + 1, 1, rows), jnp.float32),
            jax.ShapeDtypeStruct((reps, 1, length), jnp.float32),
        ],
        compiler_params=pltpu.CompilerParams(vmem_limit_bytes=DOTS_LIMIT),
        cost_estimate=pl.CostEstimate(
            flops=2 * reps * length * rows * D,
            bytes_accessed=4 * reps * length * rows,
            transcendentals=rows,
        ),
    )(scalars, *operands)


def margin_kernel(places, terms, sc_ref, *refs):
    slots = len(places)
    s_refs, p_refs, refs = refs[:slots], refs[slots : slots + terms], refs[slots + terms :]
    f_ref, e_ref, means, halves = refs
    reps, rows, lanes = s_refs[0].shape
    parts = rows // BLOCK
    planes = means.shape[0] - 1
    root = math.sqrt(D)

    @pl.when(pl.program_id(0) == 0)
    def _():
        total = p_refs[0][:, 0, :]
        for ref in p_refs[1:]:
            total = total + ref[:, 0, :]
        means[...] = (total / (K * root)).astype(jnp.bfloat16).astype(jnp.float32)
        for t, (hop, way) in enumerate(places):
            plane, _ = plane_at(sc_ref, planes, hop, way)
            row = means[pl.ds(jnp.clip(plane, 0, planes - 1), 1), :]
            halves[t] = (0.5 * root) * jnp.transpose(jnp.broadcast_to(row, (LANES, rows)))

    for e in range(reps):
        at = lax.rem(sc_ref[2] + e, reps)
        for t in range(slots):
            for b in range(parts):

                def one_line(i, top):
                    line = pl.ds(pl.multiple_of(b * BLOCK + i * 8, 8), 8)
                    half = jnp.concatenate([halves[t, line, :]] * (lanes // LANES), axis=1)
                    return jnp.maximum(top, s_refs[t][e, line, :] - half)

                top = jnp.full((8, lanes), -jnp.inf, jnp.float32)
                top = lax.fori_loop(0, BLOCK // 8, one_line, top, unroll=8)
                line = t * parts + b
                e_ref[at, line : line + 1, :] = jnp.max(top, axis=0, keepdims=True) * (1 / root)
        line = slots * parts
        e_ref[at, line : line + 1, :] = f_ref[e]
        mean = means[pl.ds(sc_ref[0], 1), :]
        for start in range(0, lanes, rows):
            e_ref[at, line + 1 : line + 2, start : start + min(rows, lanes)] = mean[:, :lanes]


def margin_call(scalars, dots, bwd_terms, fwd_parts, places, whole):
    terms, slots = len(bwd_terms), len(dots)
    reps, rows, length = dots[0].shape
    lines = -(-(slots * (rows // BLOCK) + 2) // 8) * 8
    tile = length if whole else rows
    if whole:
        s_spec = p_spec = f_spec = e_spec = pl.BlockSpec(memory_space=pltpu.VMEM)
    else:
        s_spec = pl.BlockSpec((reps, rows, tile), lambda j: (0, 0, j))
        p_spec = pl.BlockSpec(bwd_terms[0].shape, lambda j: (0, 0, 0))
        f_spec = pl.BlockSpec((reps, 1, tile), lambda j: (0, 0, j))
        e_spec = pl.BlockSpec((reps, lines, tile), lambda j: (0, 0, j))
    return pl.pallas_call(
        functools.partial(margin_kernel, places, terms),
        grid=(length // tile,),
        in_specs=[pl.BlockSpec(memory_space=pltpu.SMEM)]
        + [s_spec] * slots
        + [p_spec] * terms
        + [f_spec],
        out_specs=e_spec,
        scratch_shapes=[
            pltpu.VMEM((bwd_terms[0].shape[0], rows), jnp.float32),
            pltpu.VMEM((slots, rows, LANES), jnp.float32),
        ],
        out_shape=jax.ShapeDtypeStruct((reps, lines, length), jnp.float32),
        compiler_params=pltpu.CompilerParams(
            vmem_limit_bytes=DOTS_LIMIT if whole else VMEM_LIMIT
        ),
        cost_estimate=pl.CostEstimate(
            flops=rows * D, bytes_accessed=rows * D, transcendentals=0
        ),
    )(scalars, *dots, *bwd_terms, fwd_parts)


def final_kernel(width, reps, planes, slots, parts, sc_ref, list_ref, g_ref, best_ref, fwd_ref, bwd_ref):
    shard, wide, rep = sc_ref[0], sc_ref[1], sc_ref[2]
    both = (planes - 1) // 2
    fwd_line = slots * parts
    fwd = g_ref[0, 0, fwd_line : fwd_line + 1, :]
    for g in range(1, width * reps):
        fwd = fwd + g_ref[g, 0, fwd_line : fwd_line + 1, :]
    fwd = fwd / (K * math.sqrt(D))
    fwd_ref[...] = fwd
    rows = parts * BLOCK
    for v in range(width):
        part = g_ref[v * reps + rep, 0, fwd_line + 1 : fwd_line + 2, 0:rows]
        bwd_ref[:, v * rows : (v + 1) * rows] = part.astype(jnp.bfloat16)
    half = 0.5 * fwd
    per_width = best_ref.shape[0]
    for c in range(per_width):
        block = list_ref[wide * per_width + c]
        holder = block // (parts * width)
        local = block - holder * (parts * width)
        plane = holder // reps
        peer = (local // parts) * reps + holder - plane * reps
        hops = jnp.abs(shard - plane)
        near = 2 * hops - 1 + jnp.where(plane > shard, 1, 0)
        slot = jnp.where(hops == 0, 0, jnp.where(hops <= both, near, both + hops))
        line = slot * parts + local - (local // parts) * parts
        best_ref[c : c + 1, :] = g_ref[peer, 0, pl.ds(line, 1), :] - half


def final_call(scalars, own_list, gathered, width, reps, planes, slots, parts):
    lines, length = gathered.shape[2:]
    per_width = CAND // width
    return pl.pallas_call(
        functools.partial(final_kernel, width, reps, planes, slots, parts),
        grid_spec=pltpu.PrefetchScalarGridSpec(
            num_scalar_prefetch=2,
            grid=(1,),
            in_specs=[
                pl.BlockSpec((width * reps, 1, lines, length), lambda j, sc, ls: (0, sc[2], 0, 0))
            ],
            out_specs=[
                pl.BlockSpec((per_width, length), lambda j, sc, ls: (0, 0)),
                pl.BlockSpec((1, length), lambda j, sc, ls: (0, 0)),
                pl.BlockSpec((1, length), lambda j, sc, ls: (0, 0)),
            ],
        ),
        out_shape=[
            jax.ShapeDtypeStruct((per_width, length), jnp.float32),
            jax.ShapeDtypeStruct((1, length), jnp.float32),
            jax.ShapeDtypeStruct((1, length), jnp.bfloat16),
        ],
        compiler_params=pltpu.CompilerParams(vmem_limit_bytes=16 * MIB),
    )(scalars, own_list, gathered)


def together(*values):
    return lax.optimization_barrier(values)


def on_device(source_vecs, target_vecs, fwd_owner, fwd_row, bwd_owner, bwd_row, cand_lists):
    reps = lax.axis_size("rep")
    planes = lax.axis_size("shard")
    width = lax.axis_size("width")
    shard = lax.axis_index("shard")
    wide = lax.axis_index("width")
    rep = lax.axis_index("rep")
    length = source_vecs.shape[0]
    rows = length // width
    parts = rows // BLOCK

    def part_of(values, index, axis=0):
        return lax.dynamic_slice_in_dim(values, index * rows, rows, axis)

    def shift(values, axis, count, by):
        return lax.ppermute(values, axis, [((i + by) % count, i) for i in range(count)])

    bidx = jnp.transpose(bwd_owner * length + bwd_row)
    codes = [bidx // CODE, lax.rem(bidx, CODE), jnp.zeros((EXTRA - 2 * K, length), jnp.int32)]
    codes = jnp.concatenate(codes).astype(jnp.bfloat16)
    first = [part_of(target_vecs, wide)]
    rest = []
    for d in range(1, width):
        index = lax.rem(wide + width - d, width)
        sent = part_of(target_vecs, index)
        if d == 1:
            sent = jnp.concatenate([sent, part_of(codes, index, 1)])
        rest.append(shift(sent, "width", width, d))
    fidx_own = jnp.transpose(fwd_owner * length + fwd_row)

    def over_reps(values):
        return jnp.stack([values] + [shift(values, "rep", reps, e) for e in range(1, reps)])

    fidx = over_reps(fidx_own)

    def moved(chunks, hop):
        out = []
        half = len(chunks) // 2
        ways = (chunks, chunks) if hop == 1 else (chunks[:half], chunks[half:])
        for by, side in zip((1, -1), ways):
            pairs = [(i, i + by) for i in range(planes) if 0 <= i + by < planes]
            pairs = [(i, j) for i, j in pairs if 0 <= j - by * hop < planes]
            out += [lax.ppermute(c, "shard", pairs) for c in side]
        return out

    both = (planes - 1) // 2
    queue = [(0, "own")]
    for hop in range(1, planes):
        queue += [(hop, "up"), (hop, "down")] if hop <= both else [(hop, "one")]
    dots, places, state = [], [], None
    scalars = jnp.stack([shard, wide, rep]).astype(jnp.int32)

    heads, tails = {0: first}, {0: rest}
    for hop in range(1, planes):
        heads[hop] = moved(heads[hop - 1], hop)
        if hop < 3:
            tails[hop] = moved(tails[hop - 1], hop)
    *_, fidx, held = together(*heads[1], *rest, fidx, source_vecs)
    sources = [held] + [shift(held, "width", width, d) for d in range(1, width)]
    got = together(*sources, *tails[1], *heads[2])
    sources = list(got[:width])
    src = [normalize_rows(sources)]
    for e in range(1, reps):
        src.append(shift(src[0], "rep", reps, e))

    def arrived(hop, side):
        half = len(tails[hop]) // 2
        return [heads[hop][side]] + tails[hop][side * half : side * half + half]

    for place, (hop, way) in enumerate(queue):
        if place == AHEAD:
            own_again, state[0] = together(fidx_own, state[0])
            fidx = over_reps(own_again)
            *late, fidx = together(*tails[2], fidx)
            tails[2] = list(late)
            for later in range(3, planes):
                tails[later] = moved(tails[later - 1], later)
        if way == "own":
            chunks = [first + rest]
        else:
            sides = {"up": (0,), "down": (1,), "one": (0, 1)}[way]
            chunks = [arrived(hop, side) for side in sides]
        out, *state = dots_call(scalars, fidx, src, chunks, state, planes, hop, way)
        dots.append(out)
        places.append((hop, way))

    def over_planes(values):
        if planes > 4:
            return [lax.psum(values, "shard")]
        return [values] + [shift(values, "shard", planes, d) for d in range(1, planes)]

    lines = margin_call(
        scalars, dots, over_planes(state[0]), state[1], tuple(places), planes <= 4
    )
    gathered = lax.all_gather(lines, ("width", "rep"), axis=0, tiled=False)
    own_list = lax.dynamic_index_in_dim(cand_lists, shard, 0, keepdims=False)
    best, fwd_mean, bwd_mean = final_call(
        scalars, own_list, gathered, width, reps, planes, len(dots), parts
    )
    return (jnp.transpose(best), fwd_mean.reshape(-1), bwd_mean.reshape(-1))


def solution(mesh):
    in_specs = (
        P(("groups", "shard", "rep"), "width"),
        P(("groups", "shard", "rep"), "width"),
        P(("groups", "shard", "rep"), None),
        P(("groups", "shard", "rep"), None),
        P(("groups", "shard", "rep"), None),
        P(("groups", "shard", "rep"), None),
        P("groups", None),
    )
    out_specs = (
        P(("groups", "shard", "rep"), "width"),
        P(("groups", "shard", "rep")),
        P(("groups", "shard", "rep")),
    )
    return jax.shard_map(
        on_device, mesh=mesh, in_specs=in_specs, out_specs=out_specs, check_vma=False
    )
```

```python
import functools
import math

import jax
import jax.numpy as jnp
from jax import lax
from jax.experimental import pallas as pl
from jax.experimental.pallas import tpu as pltpu
from jax.sharding import PartitionSpec as P

D = 1024
K = 4
CAND = 16
BLOCK = 256
EPS = 1e-05
LANES = 128
TILE = 256
MIB = 1 << 20
CODE = 256
EXTRA = 16
AHEAD = 1
VMEM_LIMIT = 56 * MIB
DOTS_LIMIT = 12 * MIB


def normalize_kernel(*refs):
    chunks, out_ref = refs[:-1], refs[-1]
    cols = chunks[0].shape[1]
    values = [ref[...].astype(jnp.float32) for ref in chunks]
    total = sum(jnp.sum(v * v, axis=1, keepdims=True) for v in values)
    scale = lax.rsqrt(total / D + EPS)
    for d, v in enumerate(values):
        out_ref[:, d * cols : (d + 1) * cols] = (v * scale).astype(jnp.bfloat16)


def normalize_rows(chunks):
    rows, cols = chunks[0].shape
    return pl.pallas_call(
        normalize_kernel,
        grid=(rows // TILE,),
        in_specs=[pl.BlockSpec((TILE, cols), lambda i: (i, 0))] * len(chunks),
        out_specs=pl.BlockSpec((TILE, cols * len(chunks)), lambda i: (i, 0)),
        out_shape=jax.ShapeDtypeStruct((rows, cols * len(chunks)), jnp.bfloat16),
        compiler_params=pltpu.CompilerParams(vmem_limit_bytes=16 * MIB),
        cost_estimate=pl.CostEstimate(
            flops=rows * D, bytes_accessed=rows * D, transcendentals=rows
        ),
    )(*chunks)


def plane_at(sc_ref, planes, hop, way):
    shard = sc_ref[0]
    if way in ("own", "up"):
        plane = shard - hop
    elif way == "down":
        plane = shard + hop
    else:
        plane = jnp.where(shard >= hop, shard - hop, shard + hop)
    return plane, (plane >= 0) & (plane < planes)


def dots_kernel(reps, width, pairs, planes, hop, way, sc_ref, *refs):
    first = hop == 0
    fidx_ref, src_refs = refs[0], refs[1 : 1 + reps]
    chunk_refs = refs[1 + reps : 1 + reps + width * pairs]
    refs = refs[1 + reps + width * pairs :]
    p_in, f_in = None, None
    if not first:
        p_in, f_in, refs = refs[0], refs[1], refs[2:]
    s_ref, p_ref, f_ref, tgt, picks, bsum = refs
    rows, cols = chunk_refs[0].shape
    length = src_refs[0].shape[0]
    groups = length // LANES
    shard, wide, rep = sc_ref[0], sc_ref[1], sc_ref[2]
    plane, valid = plane_at(sc_ref, planes, hop, way)

    @pl.when(valid)
    def _():
        values = []
        for d in range(width):
            value = chunk_refs[d][...].astype(jnp.float32)
            for other in range(1, pairs):
                value = value + chunk_refs[other * width + d][...].astype(jnp.float32)
            if d == 1:
                codes = value[rows:]
                value = value[:rows]
            values.append(value)
        total = sum(jnp.sum(v * v, axis=1, keepdims=True) for v in values)
        scale = lax.rsqrt(total / D + EPS)
        for d, v in enumerate(values):
            tgt[:, d * cols : (d + 1) * cols] = (v * scale).astype(jnp.bfloat16)

        bidx = (codes[:K] * CODE + codes[K : 2 * K]).astype(jnp.int32)
        base = (plane * reps + rep) * length + wide * rows
        lane_ids = lax.broadcasted_iota(jnp.int32, (8, LANES), 1)
        row_ids = lax.broadcasted_iota(jnp.int32, (8, length), 0)
        for e in range(reps):
            place = bidx - (shard * reps + lax.rem(rep + e, reps)) * length
            hit = (place >= 0) & (place < length)
            place = jnp.sum(jnp.where(hit, place + 1, 0), axis=0, keepdims=True) - 1
            place = jnp.broadcast_to(place.astype(jnp.float32), (LANES, rows))
            picks[...] = jnp.transpose(place).astype(jnp.int32)

            s_ref[e] = lax.dot_general(
                tgt[...],
                src_refs[e][...],
                (((1,), (1,)), ((), ())),
                preferred_element_type=jnp.float32,
            )
            place = fidx_ref[e] - base
            hit = (place >= 0) & (place < rows)
            place = jnp.sum(jnp.where(hit, place + 1, 0), axis=0, keepdims=True) - 1
            away = jnp.broadcast_to(place, (8, length)) - row_ids

            def one_line(i, total):
                line = pl.ds(pl.multiple_of(i * 8, 8), 8)
                dots = s_ref[e, line, :]
                pick = picks[line, :] - lane_ids
                part = jnp.zeros((8, LANES), jnp.float32)
                for g in range(groups):
                    one = dots[:, g * LANES : (g + 1) * LANES]
                    part = part + jnp.where(pick == g * LANES, one, 0.0)
                if e > 0:
                    part = part + bsum[line, :]
                bsum[line, :] = part
                return total + jnp.where(away == i * 8, dots, 0.0)

            total = lax.fori_loop(
                0, rows // 8, one_line, jnp.zeros((8, length), jnp.float32), unroll=4
            )
            picked = jnp.sum(total, axis=0, keepdims=True)
            f_ref[e] = picked if first else f_in[e] + picked

        if not first:
            p_ref[...] = p_in[...]
        p_ref[plane] = jnp.sum(jnp.transpose(bsum[...]), axis=0, keepdims=True)

    if not first:

        @pl.when(jnp.logical_not(valid))
        def _():
            p_ref[...] = p_in[...]
            f_ref[...] = f_in[...]


def dots_call(scalars, fidx, sources, chunks, state, planes, hop, way):
    reps = len(sources)
    pairs, width = len(chunks), len(chunks[0])
    length = sources[0].shape[0]
    rows = chunks[0][0].shape[0]
    flat = [c for pair in chunks for c in pair]
    state = [] if state is None else state
    operands = [fidx, *sources, *flat, *state]
    vmem = pl.BlockSpec(memory_space=pltpu.VMEM)
    return pl.pallas_call(
        functools.partial(dots_kernel, reps, width, pairs, planes, hop, way),
        in_specs=[pl.BlockSpec(memory_space=pltpu.SMEM)] + [vmem] * len(operands),
        out_specs=[vmem] * 3,
        scratch_shapes=[
            pltpu.VMEM((rows, D), jnp.bfloat16),
            pltpu.VMEM((rows, LANES), jnp.int32),
            pltpu.VMEM((rows, LANES), jnp.float32),
        ],
        out_shape=[
            jax.ShapeDtypeStruct((reps, rows, length), jnp.float32),
            jax.ShapeDtypeStruct((planes, 1, rows), jnp.float32),
            jax.ShapeDtypeStruct((reps, 1, length), jnp.float32),
        ],
        compiler_params=pltpu.CompilerParams(vmem_limit_bytes=DOTS_LIMIT),
        cost_estimate=pl.CostEstimate(
            flops=2 * reps * length * rows * D,
            bytes_accessed=4 * reps * length * rows,
            transcendentals=rows,
        ),
    )(scalars, *operands)


def margin_kernel(places, terms, sc_ref, *refs):
    slots = len(places)
    s_refs, p_refs, refs = refs[:slots], refs[slots : slots + terms], refs[slots + terms :]
    f_ref, e_ref, means, halves = refs
    reps, rows, lanes = s_refs[0].shape
    parts = rows // BLOCK
    planes = means.shape[0]
    root = math.sqrt(D)

    @pl.when(pl.program_id(0) == 0)
    def _():
        total = p_refs[0][:, 0, :]
        for ref in p_refs[1:]:
            total = total + ref[:, 0, :]
        means[...] = (total / (K * root)).astype(jnp.bfloat16).astype(jnp.float32)
        for t, (hop, way) in enumerate(places):
            plane, _ = plane_at(sc_ref, planes, hop, way)
            row = means[pl.ds(jnp.clip(plane, 0, planes - 1), 1), :]
            halves[t] = (0.5 * root) * jnp.transpose(jnp.broadcast_to(row, (LANES, rows)))

    for e in range(reps):
        at = lax.rem(sc_ref[2] + e, reps)
        for t in range(slots):
            for b in range(parts):

                def one_line(i, top):
                    line = pl.ds(pl.multiple_of(b * BLOCK + i * 8, 8), 8)
                    half = jnp.concatenate([halves[t, line, :]] * (lanes // LANES), axis=1)
                    return jnp.maximum(top, s_refs[t][e, line, :] - half)

                top = jnp.full((8, lanes), -jnp.inf, jnp.float32)
                top = lax.fori_loop(0, BLOCK // 8, one_line, top, unroll=8)
                line = t * parts + b
                e_ref[at, line : line + 1, :] = jnp.max(top, axis=0, keepdims=True) * (1 / root)
        line = slots * parts
        e_ref[at, line : line + 1, :] = f_ref[e]
        mean = means[pl.ds(sc_ref[0], 1), :]
        for start in range(0, lanes, rows):
            e_ref[at, line + 1 : line + 2, start : start + min(rows, lanes)] = mean[:, :lanes]


def margin_call(scalars, dots, bwd_terms, fwd_parts, places, whole):
    terms, slots = len(bwd_terms), len(dots)
    reps, rows, length = dots[0].shape
    lines = -(-(slots * (rows // BLOCK) + 2) // 8) * 8
    tile = length if whole else rows
    if whole:
        s_spec = p_spec = f_spec = e_spec = pl.BlockSpec(memory_space=pltpu.VMEM)
    else:
        s_spec = pl.BlockSpec((reps, rows, tile), lambda j: (0, 0, j))
        p_spec = pl.BlockSpec(bwd_terms[0].shape, lambda j: (0, 0, 0))
        f_spec = pl.BlockSpec((reps, 1, tile), lambda j: (0, 0, j))
        e_spec = pl.BlockSpec((reps, lines, tile), lambda j: (0, 0, j))
    return pl.pallas_call(
        functools.partial(margin_kernel, places, terms),
        grid=(length // tile,),
        in_specs=[pl.BlockSpec(memory_space=pltpu.SMEM)]
        + [s_spec] * slots
        + [p_spec] * terms
        + [f_spec],
        out_specs=e_spec,
        scratch_shapes=[
            pltpu.VMEM((bwd_terms[0].shape[0], rows), jnp.float32),
            pltpu.VMEM((slots, rows, LANES), jnp.float32),
        ],
        out_shape=jax.ShapeDtypeStruct((reps, lines, length), jnp.float32),
        compiler_params=pltpu.CompilerParams(
            vmem_limit_bytes=DOTS_LIMIT if whole else VMEM_LIMIT
        ),
        cost_estimate=pl.CostEstimate(
            flops=rows * D, bytes_accessed=rows * D, transcendentals=0
        ),
    )(scalars, *dots, *bwd_terms, fwd_parts)


def final_kernel(width, reps, planes, slots, parts, sc_ref, list_ref, g_ref, best_ref, fwd_ref, bwd_ref):
    shard, wide, rep = sc_ref[0], sc_ref[1], sc_ref[2]
    both = (planes - 1) // 2
    fwd_line = slots * parts
    fwd = g_ref[0, 0, fwd_line : fwd_line + 1, :]
    for g in range(1, width * reps):
        fwd = fwd + g_ref[g, 0, fwd_line : fwd_line + 1, :]
    fwd = fwd / (K * math.sqrt(D))
    fwd_ref[...] = fwd
    rows = parts * BLOCK
    for v in range(width):
        part = g_ref[v * reps + rep, 0, fwd_line + 1 : fwd_line + 2, 0:rows]
        bwd_ref[:, v * rows : (v + 1) * rows] = part.astype(jnp.bfloat16)
    half = 0.5 * fwd
    per_width = best_ref.shape[0]
    for c in range(per_width):
        block = list_ref[wide * per_width + c]
        holder = block // (parts * width)
        local = block - holder * (parts * width)
        plane = holder // reps
        peer = (local // parts) * reps + holder - plane * reps
        hops = jnp.abs(shard - plane)
        near = 2 * hops - 1 + jnp.where(plane > shard, 1, 0)
        slot = jnp.where(hops == 0, 0, jnp.where(hops <= both, near, both + hops))
        line = slot * parts + local - (local // parts) * parts
        best_ref[c : c + 1, :] = g_ref[peer, 0, pl.ds(line, 1), :] - half


def final_call(scalars, own_list, gathered, width, reps, planes, slots, parts):
    lines, length = gathered.shape[2:]
    per_width = CAND // width
    return pl.pallas_call(
        functools.partial(final_kernel, width, reps, planes, slots, parts),
        grid_spec=pltpu.PrefetchScalarGridSpec(
            num_scalar_prefetch=2,
            grid=(1,),
            in_specs=[
                pl.BlockSpec((width * reps, 1, lines, length), lambda j, sc, ls: (0, sc[2], 0, 0))
            ],
            out_specs=[
                pl.BlockSpec((per_width, length), lambda j, sc, ls: (0, 0)),
                pl.BlockSpec((1, length), lambda j, sc, ls: (0, 0)),
                pl.BlockSpec((1, length), lambda j, sc, ls: (0, 0)),
            ],
        ),
        out_shape=[
            jax.ShapeDtypeStruct((per_width, length), jnp.float32),
            jax.ShapeDtypeStruct((1, length), jnp.float32),
            jax.ShapeDtypeStruct((1, length), jnp.bfloat16),
        ],
        compiler_params=pltpu.CompilerParams(vmem_limit_bytes=16 * MIB),
    )(scalars, own_list, gathered)


def together(*values):
    return lax.optimization_barrier(values)


def on_device(source_vecs, target_vecs, fwd_owner, fwd_row, bwd_owner, bwd_row, cand_lists):
    reps = lax.axis_size("rep")
    planes = lax.axis_size("shard")
    width = lax.axis_size("width")
    shard = lax.axis_index("shard")
    wide = lax.axis_index("width")
    rep = lax.axis_index("rep")
    length = source_vecs.shape[0]
    rows = length // width
    parts = rows // BLOCK

    def part_of(values, index, axis=0):
        return lax.dynamic_slice_in_dim(values, index * rows, rows, axis)

    def shift(values, axis, count, by):
        return lax.ppermute(values, axis, [((i + by) % count, i) for i in range(count)])

    bidx = jnp.transpose(bwd_owner * length + bwd_row)
    codes = [bidx // CODE, lax.rem(bidx, CODE), jnp.zeros((EXTRA - 2 * K, length), jnp.int32)]
    codes = jnp.concatenate(codes).astype(jnp.bfloat16)
    first = [part_of(target_vecs, wide)]
    rest = []
    for d in range(1, width):
        index = lax.rem(wide + width - d, width)
        sent = part_of(target_vecs, index)
        if d == 1:
            sent = jnp.concatenate([sent, part_of(codes, index, 1)])
        rest.append(shift(sent, "width", width, d))
    fidx_own = jnp.transpose(fwd_owner * length + fwd_row)

    def over_reps(values):
        return jnp.stack([values] + [shift(values, "rep", reps, e) for e in range(1, reps)])

    fidx = over_reps(fidx_own)

    def moved(chunks, hop):
        out = []
        half = len(chunks) // 2
        ways = (chunks, chunks) if hop == 1 else (chunks[:half], chunks[half:])
        for by, side in zip((1, -1), ways):
            pairs = [(i, i + by) for i in range(planes) if 0 <= i + by < planes]
            pairs = [(i, j) for i, j in pairs if 0 <= j - by * hop < planes]
            out += [lax.ppermute(c, "shard", pairs) for c in side]
        return out

    both = (planes - 1) // 2
    queue = [(0, "own")]
    for hop in range(1, planes):
        queue += [(hop, "up"), (hop, "down")] if hop <= both else [(hop, "one")]
    dots, places, state = [], [], None
    scalars = jnp.stack([shard, wide, rep]).astype(jnp.int32)

    heads, tails = {0: first}, {0: rest}
    for hop in range(1, planes):
        heads[hop] = moved(heads[hop - 1], hop)
        if hop < 3:
            tails[hop] = moved(tails[hop - 1], hop)
    *_, fidx, held = together(*rest, fidx, source_vecs)
    sources = [held] + [shift(held, "width", width, d) for d in range(1, width)]
    got = together(*sources, *tails[1], *heads[2])
    sources = list(got[:width])
    src = [normalize_rows(sources)]
    for e in range(1, reps):
        src.append(shift(src[0], "rep", reps, e))

    def arrived(hop, side):
        half = len(tails[hop]) // 2
        return [heads[hop][side]] + tails[hop][side * half : side * half + half]

    for place, (hop, way) in enumerate(queue):
        if place == AHEAD:
            own_again, state[0] = together(fidx_own, state[0])
            fidx = over_reps(own_again)
            *late, fidx = together(*tails[2], fidx)
            tails[2] = list(late)
            for later in range(3, planes):
                tails[later] = moved(tails[later - 1], later)
        if way == "own":
            chunks = [first + rest]
        else:
            sides = {"up": (0,), "down": (1,), "one": (0, 1)}[way]
            chunks = [arrived(hop, side) for side in sides]
        out, *state = dots_call(scalars, fidx, src, chunks, state, planes, hop, way)
        dots.append(out)
        places.append((hop, way))

    def over_planes(values):
        if planes > 4:
            return [lax.psum(values, "shard")]
        return [values] + [shift(values, "shard", planes, d) for d in range(1, planes)]

    lines = margin_call(
        scalars, dots, over_planes(state[0]), state[1], tuple(places), planes <= 4
    )
    gathered = lax.all_gather(lines, ("width", "rep"), axis=0, tiled=False)
    own_list = lax.dynamic_index_in_dim(cand_lists, shard, 0, keepdims=False)
    best, fwd_mean, bwd_mean = final_call(
        scalars, own_list, gathered, width, reps, planes, len(dots), parts
    )
    return (jnp.transpose(best), fwd_mean.reshape(-1), bwd_mean.reshape(-1))


def solution(mesh):
    in_specs = (
        P(("groups", "shard", "rep"), "width"),
        P(("groups", "shard", "rep"), "width"),
        P(("groups", "shard", "rep"), None),
        P(("groups", "shard", "rep"), None),
        P(("groups", "shard", "rep"), None),
        P(("groups", "shard", "rep"), None),
        P("groups", None),
    )
    out_specs = (
        P(("groups", "shard", "rep"), "width"),
        P(("groups", "shard", "rep")),
        P(("groups", "shard", "rep")),
    )
    return jax.shard_map(
        on_device, mesh=mesh, in_specs=in_specs, out_specs=out_specs, check_vma=False
    )
```

```python
import functools
import math

import jax
import jax.numpy as jnp
from jax import lax
from jax.experimental import pallas as pl
from jax.experimental.pallas import tpu as pltpu
from jax.sharding import PartitionSpec as P

D = 1024
K = 4
CAND = 16
BLOCK = 256
EPS = 1e-05
LANES = 128
TILE = 256
MIB = 1 << 20
CODE = 256
EXTRA = 16
AHEAD = 1
VMEM_LIMIT = 56 * MIB
DOTS_LIMIT = 12 * MIB


def normalize_kernel(*refs):
    chunks, out_ref = refs[:-1], refs[-1]
    cols = chunks[0].shape[1]
    values = [ref[...].astype(jnp.float32) for ref in chunks]
    total = sum(jnp.sum(v * v, axis=1, keepdims=True) for v in values)
    scale = lax.rsqrt(total / D + EPS)
    for d, v in enumerate(values):
        out_ref[:, d * cols : (d + 1) * cols] = (v * scale).astype(jnp.bfloat16)


def normalize_rows(chunks):
    rows, cols = chunks[0].shape
    return pl.pallas_call(
        normalize_kernel,
        grid=(rows // TILE,),
        in_specs=[pl.BlockSpec((TILE, cols), lambda i: (i, 0))] * len(chunks),
        out_specs=pl.BlockSpec((TILE, cols * len(chunks)), lambda i: (i, 0)),
        out_shape=jax.ShapeDtypeStruct((rows, cols * len(chunks)), jnp.bfloat16),
        compiler_params=pltpu.CompilerParams(vmem_limit_bytes=16 * MIB),
        cost_estimate=pl.CostEstimate(
            flops=rows * D, bytes_accessed=rows * D, transcendentals=rows
        ),
    )(*chunks)


def plane_at(sc_ref, planes, hop, way):
    shard = sc_ref[0]
    if way in ("own", "up"):
        plane = shard - hop
    elif way == "down":
        plane = shard + hop
    else:
        plane = jnp.where(shard >= hop, shard - hop, shard + hop)
    return plane, (plane >= 0) & (plane < planes)


def dots_of(sc_ref, fidx_ref, src_refs, chunk_refs, width, planes, hop, way, outs):
    s_ref, p_ref, f_ref, tgt, picks, bsum = outs
    first = hop == 0
    reps, pairs = len(src_refs), len(chunk_refs) // width
    rows, cols = chunk_refs[0].shape
    length = src_refs[0].shape[0]
    groups = length // LANES
    shard, wide, rep = sc_ref[0], sc_ref[1], sc_ref[2]
    plane, valid = plane_at(sc_ref, planes, hop, way)

    @pl.when(valid)
    def _():
        values = []
        for d in range(width):
            value = chunk_refs[d][...].astype(jnp.float32)
            for other in range(1, pairs):
                value = value + chunk_refs[other * width + d][...].astype(jnp.float32)
            if d == 1:
                codes = value[rows:]
                value = value[:rows]
            values.append(value)
        total = sum(jnp.sum(v * v, axis=1, keepdims=True) for v in values)
        scale = lax.rsqrt(total / D + EPS)
        for d, v in enumerate(values):
            tgt[:, d * cols : (d + 1) * cols] = (v * scale).astype(jnp.bfloat16)

        bidx = (codes[:K] * CODE + codes[K : 2 * K]).astype(jnp.int32)
        base = (plane * reps + rep) * length + wide * rows
        lane_ids = lax.broadcasted_iota(jnp.int32, (8, LANES), 1)
        row_ids = lax.broadcasted_iota(jnp.int32, (8, length), 0)
        for e in range(reps):
            place = bidx - (shard * reps + lax.rem(rep + e, reps)) * length
            hit = (place >= 0) & (place < length)
            place = jnp.sum(jnp.where(hit, place + 1, 0), axis=0, keepdims=True) - 1
            place = jnp.broadcast_to(place.astype(jnp.float32), (LANES, rows))
            picks[...] = jnp.transpose(place).astype(jnp.int32)

            s_ref[e] = lax.dot_general(
                tgt[...],
                src_refs[e][...],
                (((1,), (1,)), ((), ())),
                preferred_element_type=jnp.float32,
            )
            place = fidx_ref[e] - base
            hit = (place >= 0) & (place < rows)
            place = jnp.sum(jnp.where(hit, place + 1, 0), axis=0, keepdims=True) - 1
            away = jnp.broadcast_to(place, (8, length)) - row_ids

            def one_line(i, total):
                line = pl.ds(pl.multiple_of(i * 8, 8), 8)
                dots = s_ref[e, line, :]
                pick = picks[line, :] - lane_ids
                part = jnp.zeros((8, LANES), jnp.float32)
                for g in range(groups):
                    one = dots[:, g * LANES : (g + 1) * LANES]
                    part = part + jnp.where(pick == g * LANES, one, 0.0)
                if e > 0:
                    part = part + bsum[line, :]
                bsum[line, :] = part
                return total + jnp.where(away == i * 8, dots, 0.0)

            total = lax.fori_loop(
                0, rows // 8, one_line, jnp.zeros((8, length), jnp.float32), unroll=4
            )
            picked = jnp.sum(total, axis=0, keepdims=True)
            f_ref[e] = picked if first else f_ref[e] + picked

        p_ref[plane] = jnp.sum(jnp.transpose(bsum[...]), axis=0, keepdims=True)


def dots_kernel(reps, width, planes, entries, sc_ref, *refs):
    fidx_ref, src_refs, refs = refs[0], refs[1 : 1 + reps], refs[1 + reps :]
    chunk_refs = []
    for _, _, pairs in entries:
        chunk_refs.append(refs[: width * pairs])
        refs = refs[width * pairs :]
    first = entries[0][0] == 0
    if not first:
        p_in, f_in, refs = refs[0], refs[1], refs[2:]
    s_refs, (p_ref, f_ref, *scratch) = refs[: len(entries)], refs[len(entries) :]
    if not first:
        p_ref[...] = p_in[...]
        f_ref[...] = f_in[...]
    for (hop, way, _), chunks, s_ref in zip(entries, chunk_refs, s_refs):
        outs = (s_ref, p_ref, f_ref, *scratch)
        dots_of(sc_ref, fidx_ref, src_refs, chunks, width, planes, hop, way, outs)


def dots_call(scalars, fidx, sources, parts, state, planes):
    reps = len(sources)
    length = sources[0].shape[0]
    width = len(parts[0][2][0])
    rows = length // width
    flat = [c for _, _, chunks in parts for pair in chunks for c in pair]
    entries = [(hop, way, len(chunks)) for hop, way, chunks in parts]
    state = [] if state is None else state
    operands = [fidx, *sources, *flat, *state]
    vmem = pl.BlockSpec(memory_space=pltpu.VMEM)
    count = len(parts)
    heavy = 0 if parts[0][0] == 0 else count
    *dots, p, f = pl.pallas_call(
        functools.partial(dots_kernel, reps, width, planes, entries),
        in_specs=[pl.BlockSpec(memory_space=pltpu.SMEM)] + [vmem] * len(operands),
        out_specs=[vmem] * (count + 2),
        scratch_shapes=[
            pltpu.VMEM((rows, D), jnp.bfloat16),
            pltpu.VMEM((rows, LANES), jnp.int32),
            pltpu.VMEM((rows, LANES), jnp.float32),
        ],
        out_shape=[jax.ShapeDtypeStruct((reps, rows, length), jnp.float32)] * count
        + [
            jax.ShapeDtypeStruct((planes, 1, rows), jnp.float32),
            jax.ShapeDtypeStruct((reps, 1, length), jnp.float32),
        ],
        compiler_params=pltpu.CompilerParams(vmem_limit_bytes=DOTS_LIMIT),
        cost_estimate=pl.CostEstimate(
            flops=(1 + 2 * reps * length * heavy) * rows * D,
            bytes_accessed=(D + 4 * reps * length * heavy) * rows,
            transcendentals=rows,
        ),
    )(scalars, *operands)
    return dots, [p, f]


def margin_kernel(places, terms, width, sc_ref, list_ref, *refs):
    slots = len(places)
    s_refs, p_refs, refs = refs[:slots], refs[slots : slots + terms], refs[slots + terms :]
    count = width * refs[0].shape[0]
    f_ref, outs, (e_ref, means, halves, peers, rows_of) = refs[0], refs[1 : 1 + count], refs[1 + count :]
    reps, rows, lanes = s_refs[0].shape
    parts = rows // BLOCK
    planes = means.shape[0]
    root = math.sqrt(D)

    @pl.when(pl.program_id(0) == 0)
    def _():
        total = p_refs[0][:, 0, :]
        for ref in p_refs[1:]:
            total = total + ref[:, 0, :]
        means[...] = (total / (K * root)).astype(jnp.bfloat16).astype(jnp.float32)
        for t, (hop, way) in enumerate(places):
            plane, _ = plane_at(sc_ref, planes, hop, way)
            row = means[pl.ds(jnp.clip(plane, 0, planes - 1), 1), :]
            halves[t] = (0.5 * root) * jnp.transpose(jnp.broadcast_to(row, (LANES, rows)))

    shard, wide, rep = sc_ref[0], sc_ref[1], sc_ref[2]
    both = (planes - 1) // 2
    for c in range(CAND):
        block = list_ref[c]
        holder = block // (parts * width)
        local = block - holder * (parts * width)
        plane = holder // reps
        hops = jnp.abs(shard - plane)
        near = 2 * hops - 1 + jnp.where(plane > shard, 1, 0)
        slot = jnp.where(hops == 0, 0, jnp.where(hops <= both, near, both + hops))
        peers[c] = (local // parts) * reps + holder - plane * reps
        rows_of[c] = slot * parts + local - (local // parts) * parts

    for e in range(reps):
        at = lax.rem(sc_ref[2] + e, reps)
        for t in range(slots):
            for b in range(parts):

                def one_line(i, top):
                    line = pl.ds(pl.multiple_of(b * BLOCK + i * 8, 8), 8)
                    half = jnp.concatenate([halves[t, line, :]] * (lanes // LANES), axis=1)
                    return jnp.maximum(top, s_refs[t][e, line, :] - half)

                top = jnp.full((8, lanes), -jnp.inf, jnp.float32)
                top = lax.fori_loop(0, BLOCK // 8, one_line, top, unroll=8)
                line = t * parts + b
                e_ref[at, line : line + 1, :] = jnp.max(top, axis=0, keepdims=True) * (1 / root)
        line = slots * parts
        e_ref[at, line : line + 1, :] = f_ref[e]
        mean = means[pl.ds(sc_ref[0], 1), :]
        for start in range(0, lanes, rows):
            e_ref[at, line + 1 : line + 2, start : start + min(rows, lanes)] = mean[:, :lanes]

    own = wide * reps + rep
    each = CAND // width
    line = slots * parts
    for d, out_ref in enumerate(outs):
        dest = lax.rem(own + count - d, count)
        dest_wide = dest // reps
        dest_rep = dest - dest_wide * reps
        for c in range(each):
            at = dest_wide * each + c
            row = e_ref[dest_rep, pl.ds(rows_of[at], 1), :]
            out_ref[c : c + 1, :] = jnp.where(peers[at] == own, row, 0.0)
        out_ref[each : each + 1, :] = e_ref[dest_rep, line : line + 1, :]
        for v in range(width):
            row = e_ref[dest_rep, line + 1 : line + 2, :]
            mine = (wide == v) & (dest_rep == rep)
            out_ref[each + 1 + v : each + 2 + v, :] = jnp.where(mine, row, 0.0)


def margin_call(scalars, own_list, dots, bwd_terms, fwd_parts, places, width, whole):
    terms, slots = len(bwd_terms), len(dots)
    reps, rows, length = dots[0].shape
    lines = -(-(slots * (rows // BLOCK) + 2) // 8) * 8
    tile = length if whole else rows
    count, taken = width * reps, -(-(CAND // width + 1 + width) // 8) * 8
    smem = pl.BlockSpec(memory_space=pltpu.SMEM)
    if whole:
        s_spec = p_spec = f_spec = e_spec = pl.BlockSpec(memory_space=pltpu.VMEM)
    else:
        s_spec = pl.BlockSpec((reps, rows, tile), lambda j: (0, 0, j))
        p_spec = pl.BlockSpec(bwd_terms[0].shape, lambda j: (0, 0, 0))
        f_spec = pl.BlockSpec((reps, 1, tile), lambda j: (0, 0, j))
        e_spec = pl.BlockSpec((taken, tile), lambda j: (0, j))
    return pl.pallas_call(
        functools.partial(margin_kernel, places, terms, width),
        grid=(length // tile,),
        in_specs=[smem, smem]
        + [s_spec] * slots
        + [p_spec] * terms
        + [f_spec],
        out_specs=[e_spec] * count,
        scratch_shapes=[
            pltpu.VMEM((reps, lines, tile), jnp.float32),
            pltpu.VMEM((bwd_terms[0].shape[0], rows), jnp.float32),
            pltpu.VMEM((slots, rows, LANES), jnp.float32),
            pltpu.SMEM((CAND,), jnp.int32),
            pltpu.SMEM((CAND,), jnp.int32),
        ],
        out_shape=[jax.ShapeDtypeStruct((taken, length), jnp.float32)] * count,
        compiler_params=pltpu.CompilerParams(
            vmem_limit_bytes=DOTS_LIMIT if whole else VMEM_LIMIT
        ),
        cost_estimate=pl.CostEstimate(
            flops=rows * D, bytes_accessed=rows * D, transcendentals=0
        ),
    )(scalars, own_list, *dots, *bwd_terms, fwd_parts)


def final_kernel(width, *refs):
    taken, (best_ref, fwd_ref, bwd_ref) = refs[:-3], refs[-3:]
    total = taken[0][...]
    for ref in taken[1:]:
        total = total + ref[...]
    each, length = best_ref.shape
    rows = length // width
    fwd = total[each : each + 1] / (K * math.sqrt(D))
    fwd_ref[...] = fwd
    for v in range(width):
        part = total[each + 1 + v : each + 2 + v, 0:rows]
        bwd_ref[:, v * rows : (v + 1) * rows] = part.astype(jnp.bfloat16)
    best_ref[...] = total[:each] - 0.5 * fwd


def final_call(taken, width):
    length = taken[0].shape[1]
    vmem = pl.BlockSpec(memory_space=pltpu.VMEM)
    return pl.pallas_call(
        functools.partial(final_kernel, width),
        in_specs=[vmem] * len(taken),
        out_specs=[vmem] * 3,
        out_shape=[
            jax.ShapeDtypeStruct((CAND // width, length), jnp.float32),
            jax.ShapeDtypeStruct((1, length), jnp.float32),
            jax.ShapeDtypeStruct((1, length), jnp.bfloat16),
        ],
        compiler_params=pltpu.CompilerParams(vmem_limit_bytes=16 * MIB),
    )(*taken)


def together(*values):
    return lax.optimization_barrier(values)


def on_device(source_vecs, target_vecs, fwd_owner, fwd_row, bwd_owner, bwd_row, cand_lists):
    reps = lax.axis_size("rep")
    planes = lax.axis_size("shard")
    width = lax.axis_size("width")
    shard = lax.axis_index("shard")
    wide = lax.axis_index("width")
    rep = lax.axis_index("rep")
    length = source_vecs.shape[0]
    rows = length // width
    parts = rows // BLOCK

    def part_of(values, index, axis=0):
        return lax.dynamic_slice_in_dim(values, index * rows, rows, axis)

    def shift(values, axis, count, by):
        return lax.ppermute(values, axis, [((i + by) % count, i) for i in range(count)])

    bidx = jnp.transpose(bwd_owner * length + bwd_row)
    codes = [bidx // CODE, lax.rem(bidx, CODE), jnp.zeros((EXTRA - 2 * K, length), jnp.int32)]
    codes = jnp.concatenate(codes).astype(jnp.bfloat16)
    first = [part_of(target_vecs, wide)]
    rest = []
    for d in range(1, width):
        index = lax.rem(wide + width - d, width)
        sent = part_of(target_vecs, index)
        if d == 1:
            sent = jnp.concatenate([sent, part_of(codes, index, 1)])
        rest.append(shift(sent, "width", width, d))
    fidx_own = jnp.transpose(fwd_owner * length + fwd_row)

    def over_reps(values):
        return jnp.stack([values] + [shift(values, "rep", reps, e) for e in range(1, reps)])

    fidx = over_reps(fidx_own)

    def moved(chunks, hop):
        out = []
        half = len(chunks) // 2
        ways = (chunks, chunks) if hop == 1 else (chunks[:half], chunks[half:])
        for by, side in zip((1, -1), ways):
            pairs = [(i, i + by) for i in range(planes) if 0 <= i + by < planes]
            pairs = [(i, j) for i, j in pairs if 0 <= j - by * hop < planes]
            out += [lax.ppermute(c, "shard", pairs) for c in side]
        return out

    both = (planes - 1) // 2
    queue = [(0, "own")]
    for hop in range(1, planes):
        queue += [(hop, "up"), (hop, "down")] if hop <= both else [(hop, "one")]
    dots, places, state, waiting = [], [], None, []
    scalars = jnp.stack([shard, wide, rep]).astype(jnp.int32)

    heads, tails = {0: first}, {0: rest}
    for hop in range(1, planes):
        heads[hop] = moved(heads[hop - 1], hop)
        if hop < 3:
            tails[hop] = moved(tails[hop - 1], hop)
    *_, fidx, held = together(*rest, fidx, source_vecs)
    sources = [held] + [shift(held, "width", width, d) for d in range(1, width)]
    got = together(*sources, *tails[1], *heads[2])
    sources = list(got[:width])
    src = [normalize_rows(sources)]
    for e in range(1, reps):
        src.append(shift(src[0], "rep", reps, e))

    def arrived(hop, side):
        half = len(tails[hop]) // 2
        return [heads[hop][side]] + tails[hop][side * half : side * half + half]

    for place, (hop, way) in enumerate(queue):
        if place == AHEAD:
            own_again, state[0] = together(fidx_own, state[0])
            fidx = over_reps(own_again)
            *late, fidx = together(*tails[2], fidx)
            tails[2] = list(late)
            for later in range(3, planes):
                tails[later] = moved(tails[later - 1], later)
        if way == "own":
            chunks = [first + rest]
        else:
            sides = {"up": (0,), "down": (1,), "one": (0, 1)}[way]
            chunks = [arrived(hop, side) for side in sides]
        waiting.append((hop, way, chunks))
        if place == 0 or place >= len(queue) - 2 or len(waiting) == 3:
            out, state = dots_call(scalars, fidx, src, waiting, state, planes)
            dots += out
            places += [(hop, way) for hop, way, _ in waiting]
            waiting = []

    def over_planes(values):
        if planes > 4:
            return [lax.psum(values, "shard")]
        return [values] + [shift(values, "shard", planes, d) for d in range(1, planes)]

    own_list = lax.dynamic_index_in_dim(cand_lists, shard, 0, keepdims=False)
    outs = margin_call(
        scalars, own_list, dots, over_planes(state[0]), state[1], tuple(places), width, planes <= 4
    )
    taken = [outs[0]]
    for d in range(1, width * reps):
        taken.append(shift(outs[d], ("width", "rep"), width * reps, d))
    best, fwd_mean, bwd_mean = final_call(taken, width)
    return (jnp.transpose(best), fwd_mean.reshape(-1), bwd_mean.reshape(-1))


def solution(mesh):
    in_specs = (
        P(("groups", "shard", "rep"), "width"),
        P(("groups", "shard", "rep"), "width"),
        P(("groups", "shard", "rep"), None),
        P(("groups", "shard", "rep"), None),
        P(("groups", "shard", "rep"), None),
        P(("groups", "shard", "rep"), None),
        P("groups", None),
    )
    out_specs = (
        P(("groups", "shard", "rep"), "width"),
        P(("groups", "shard", "rep")),
        P(("groups", "shard", "rep")),
    )
    return jax.shard_map(
        on_device, mesh=mesh, in_specs=in_specs, out_specs=out_specs, check_vma=False
    )
```

```python
import functools
import math

import jax
import jax.numpy as jnp
from jax import lax
from jax.experimental import pallas as pl
from jax.experimental.pallas import tpu as pltpu
from jax.sharding import PartitionSpec as P

D = 1024
K = 4
CAND = 16
BLOCK = 256
EPS = 1e-05
LANES = 128
TILE = 256
MIB = 1 << 20
CODE = 256
EXTRA = 16
AHEAD = 1
VMEM_LIMIT = 56 * MIB
DOTS_LIMIT = 12 * MIB


def normalize_kernel(*refs):
    chunks, out_ref = refs[:-1], refs[-1]
    cols = chunks[0].shape[1]
    values = [ref[...].astype(jnp.float32) for ref in chunks]
    total = sum(jnp.sum(v * v, axis=1, keepdims=True) for v in values)
    scale = lax.rsqrt(total / D + EPS)
    for d, v in enumerate(values):
        out_ref[:, d * cols : (d + 1) * cols] = (v * scale).astype(jnp.bfloat16)


def normalize_rows(chunks):
    rows, cols = chunks[0].shape
    return pl.pallas_call(
        normalize_kernel,
        grid=(rows // TILE,),
        in_specs=[pl.BlockSpec((TILE, cols), lambda i: (i, 0))] * len(chunks),
        out_specs=pl.BlockSpec((TILE, cols * len(chunks)), lambda i: (i, 0)),
        out_shape=jax.ShapeDtypeStruct((rows, cols * len(chunks)), jnp.bfloat16),
        compiler_params=pltpu.CompilerParams(vmem_limit_bytes=16 * MIB),
        cost_estimate=pl.CostEstimate(
            flops=rows * D, bytes_accessed=rows * D, transcendentals=rows
        ),
    )(*chunks)


def plane_at(sc_ref, planes, hop, way):
    shard = sc_ref[0]
    if way in ("own", "up"):
        plane = shard - hop
    elif way == "down":
        plane = shard + hop
    else:
        plane = jnp.where(shard >= hop, shard - hop, shard + hop)
    return plane, (plane >= 0) & (plane < planes)


def dots_of(sc_ref, fidx_ref, src_refs, chunk_refs, width, planes, hop, way, outs):
    s_ref, p_ref, f_ref, tgt, picks, bsum = outs
    first = hop == 0
    reps, pairs = len(src_refs), len(chunk_refs) // width
    rows, cols = chunk_refs[0].shape
    length = src_refs[0].shape[0]
    groups = length // LANES
    shard, wide, rep = sc_ref[0], sc_ref[1], sc_ref[2]
    plane, valid = plane_at(sc_ref, planes, hop, way)

    @pl.when(valid)
    def _():
        values = []
        for d in range(width):
            value = chunk_refs[d][...].astype(jnp.float32)
            for other in range(1, pairs):
                value = value + chunk_refs[other * width + d][...].astype(jnp.float32)
            if d == 1:
                codes = value[rows:]
                value = value[:rows]
            values.append(value)
        total = sum(jnp.sum(v * v, axis=1, keepdims=True) for v in values)
        scale = lax.rsqrt(total / D + EPS)
        for d, v in enumerate(values):
            tgt[:, d * cols : (d + 1) * cols] = (v * scale).astype(jnp.bfloat16)

        bidx = (codes[:K] * CODE + codes[K : 2 * K]).astype(jnp.int32)
        base = (plane * reps + rep) * length + wide * rows
        lane_ids = lax.broadcasted_iota(jnp.int32, (8, LANES), 1)
        row_ids = lax.broadcasted_iota(jnp.int32, (8, length), 0)
        for e in range(reps):
            place = bidx - (shard * reps + lax.rem(rep + e, reps)) * length
            hit = (place >= 0) & (place < length)
            place = jnp.sum(jnp.where(hit, place + 1, 0), axis=0, keepdims=True) - 1
            place = jnp.broadcast_to(place.astype(jnp.float32), (LANES, rows))
            picks[...] = jnp.transpose(place).astype(jnp.int32)

            s_ref[e] = lax.dot_general(
                tgt[...],
                src_refs[e][...],
                (((1,), (1,)), ((), ())),
                preferred_element_type=jnp.float32,
            )
            place = fidx_ref[e] - base
            hit = (place >= 0) & (place < rows)
            place = jnp.sum(jnp.where(hit, place + 1, 0), axis=0, keepdims=True) - 1
            away = jnp.broadcast_to(place, (8, length)) - row_ids

            def one_line(i, total):
                line = pl.ds(pl.multiple_of(i * 8, 8), 8)
                dots = s_ref[e, line, :]
                pick = picks[line, :] - lane_ids
                part = jnp.zeros((8, LANES), jnp.float32)
                for g in range(groups):
                    one = dots[:, g * LANES : (g + 1) * LANES]
                    part = part + jnp.where(pick == g * LANES, one, 0.0)
                if e > 0:
                    part = part + bsum[line, :]
                bsum[line, :] = part
                return total + jnp.where(away == i * 8, dots, 0.0)

            total = lax.fori_loop(
                0, rows // 8, one_line, jnp.zeros((8, length), jnp.float32), unroll=4
            )
            picked = jnp.sum(total, axis=0, keepdims=True)
            f_ref[e] = picked if first else f_ref[e] + picked

        p_ref[plane] = jnp.sum(jnp.transpose(bsum[...]), axis=0, keepdims=True)


def dots_kernel(reps, width, planes, entries, sc_ref, *refs):
    fidx_ref, src_refs, refs = refs[0], refs[1 : 1 + reps], refs[1 + reps :]
    chunk_refs = []
    for _, _, pairs in entries:
        chunk_refs.append(refs[: width * pairs])
        refs = refs[width * pairs :]
    first = entries[0][0] == 0
    if not first:
        p_in, f_in, refs = refs[0], refs[1], refs[2:]
    s_refs, (p_ref, f_ref, *scratch) = refs[: len(entries)], refs[len(entries) :]
    if not first:
        p_ref[...] = p_in[...]
        f_ref[...] = f_in[...]
    for (hop, way, _), chunks, s_ref in zip(entries, chunk_refs, s_refs):
        outs = (s_ref, p_ref, f_ref, *scratch)
        dots_of(sc_ref, fidx_ref, src_refs, chunks, width, planes, hop, way, outs)


def dots_call(scalars, fidx, sources, parts, state, planes):
    reps = len(sources)
    length = sources[0].shape[0]
    width = len(parts[0][2][0])
    rows = length // width
    flat = [c for _, _, chunks in parts for pair in chunks for c in pair]
    entries = [(hop, way, len(chunks)) for hop, way, chunks in parts]
    state = [] if state is None else state
    operands = [fidx, *sources, *flat, *state]
    vmem = pl.BlockSpec(memory_space=pltpu.VMEM)
    count = len(parts)
    heavy = 0 if parts[0][0] == 0 else count
    *dots, p, f = pl.pallas_call(
        functools.partial(dots_kernel, reps, width, planes, entries),
        in_specs=[pl.BlockSpec(memory_space=pltpu.SMEM)] + [vmem] * len(operands),
        out_specs=[vmem] * (count + 2),
        scratch_shapes=[
            pltpu.VMEM((rows, D), jnp.bfloat16),
            pltpu.VMEM((rows, LANES), jnp.int32),
            pltpu.VMEM((rows, LANES), jnp.float32),
        ],
        out_shape=[jax.ShapeDtypeStruct((reps, rows, length), jnp.float32)] * count
        + [
            jax.ShapeDtypeStruct((planes, 1, rows), jnp.float32),
            jax.ShapeDtypeStruct((reps, 1, length), jnp.float32),
        ],
        compiler_params=pltpu.CompilerParams(vmem_limit_bytes=DOTS_LIMIT),
        cost_estimate=pl.CostEstimate(
            flops=(1 + 2 * reps * length * heavy) * rows * D,
            bytes_accessed=(D + 4 * reps * length * heavy) * rows,
            transcendentals=rows,
        ),
    )(scalars, *operands)
    return dots, [p, f]


def margin_kernel(places, terms, width, sc_ref, list_ref, *refs):
    slots = len(places)
    s_refs, p_refs, refs = refs[:slots], refs[slots : slots + terms], refs[slots + terms :]
    count = width * refs[0].shape[0]
    f_ref, outs, (e_ref, means, halves, peers, rows_of) = refs[0], refs[1 : 1 + count], refs[1 + count :]
    reps, rows, lanes = s_refs[0].shape
    parts = rows // BLOCK
    planes = means.shape[0]
    root = math.sqrt(D)

    @pl.when(pl.program_id(0) == 0)
    def _():
        total = p_refs[0][:, 0, :]
        for ref in p_refs[1:]:
            total = total + ref[:, 0, :]
        means[...] = (total / (K * root)).astype(jnp.bfloat16).astype(jnp.float32)
        for t, (hop, way) in enumerate(places):
            plane, _ = plane_at(sc_ref, planes, hop, way)
            row = means[pl.ds(jnp.clip(plane, 0, planes - 1), 1), :]
            halves[t] = (0.5 * root) * jnp.transpose(jnp.broadcast_to(row, (LANES, rows)))

    shard, wide, rep = sc_ref[0], sc_ref[1], sc_ref[2]
    both = (planes - 1) // 2
    for c in range(CAND):
        block = list_ref[c]
        holder = block // (parts * width)
        local = block - holder * (parts * width)
        plane = holder // reps
        hops = jnp.abs(shard - plane)
        near = 2 * hops - 1 + jnp.where(plane > shard, 1, 0)
        slot = jnp.where(hops == 0, 0, jnp.where(hops <= both, near, both + hops))
        peers[c] = (local // parts) * reps + holder - plane * reps
        rows_of[c] = slot * parts + local - (local // parts) * parts

    for e in range(reps):
        at = lax.rem(sc_ref[2] + e, reps)
        for t in range(slots):
            for b in range(parts):

                def one_line(i, top):
                    line = pl.ds(pl.multiple_of(b * BLOCK + i * 8, 8), 8)
                    half = jnp.concatenate([halves[t, line, :]] * (lanes // LANES), axis=1)
                    return jnp.maximum(top, s_refs[t][e, line, :] - half)

                top = jnp.full((8, lanes), -jnp.inf, jnp.float32)
                top = lax.fori_loop(0, BLOCK // 8, one_line, top, unroll=8)
                line = t * parts + b
                e_ref[at, line : line + 1, :] = jnp.max(top, axis=0, keepdims=True) * (1 / root)
        line = slots * parts
        e_ref[at, line : line + 1, :] = f_ref[e]
        mean = means[pl.ds(sc_ref[0], 1), :]
        for start in range(0, lanes, rows):
            e_ref[at, line + 1 : line + 2, start : start + min(rows, lanes)] = mean[:, :lanes]

    own = wide * reps + rep
    each = CAND // width
    line = slots * parts
    for d, out_ref in enumerate(outs):
        dest = lax.rem(own + count - d, count)
        dest_wide = dest // reps
        dest_rep = dest - dest_wide * reps
        for c in range(each):
            at = dest_wide * each + c
            row = e_ref[dest_rep, pl.ds(rows_of[at], 1), :]
            out_ref[c : c + 1, :] = jnp.where(peers[at] == own, row, 0.0)
        out_ref[each : each + 1, :] = e_ref[dest_rep, line : line + 1, :]
        for v in range(width):
            row = e_ref[dest_rep, line + 1 : line + 2, :]
            mine = (wide == v) & (dest_rep == rep)
            out_ref[each + 1 + v : each + 2 + v, :] = jnp.where(mine, row, 0.0)


def margin_call(scalars, own_list, dots, bwd_terms, fwd_parts, places, width, whole):
    terms, slots = len(bwd_terms), len(dots)
    reps, rows, length = dots[0].shape
    lines = -(-(slots * (rows // BLOCK) + 2) // 8) * 8
    tile = length if whole else rows
    count, taken = width * reps, -(-(CAND // width + 1 + width) // 8) * 8
    smem = pl.BlockSpec(memory_space=pltpu.SMEM)
    if whole:
        s_spec = p_spec = f_spec = e_spec = pl.BlockSpec(memory_space=pltpu.VMEM)
    else:
        s_spec = pl.BlockSpec((reps, rows, tile), lambda j: (0, 0, j))
        p_spec = pl.BlockSpec(bwd_terms[0].shape, lambda j: (0, 0, 0))
        f_spec = pl.BlockSpec((reps, 1, tile), lambda j: (0, 0, j))
        e_spec = pl.BlockSpec((taken, tile), lambda j: (0, j))
    return pl.pallas_call(
        functools.partial(margin_kernel, places, terms, width),
        grid=(length // tile,),
        in_specs=[smem, smem]
        + [s_spec] * slots
        + [p_spec] * terms
        + [f_spec],
        out_specs=[e_spec] * count,
        scratch_shapes=[
            pltpu.VMEM((reps, lines, tile), jnp.float32),
            pltpu.VMEM((bwd_terms[0].shape[0], rows), jnp.float32),
            pltpu.VMEM((slots, rows, LANES), jnp.float32),
            pltpu.SMEM((CAND,), jnp.int32),
            pltpu.SMEM((CAND,), jnp.int32),
        ],
        out_shape=[jax.ShapeDtypeStruct((taken, length), jnp.float32)] * count,
        compiler_params=pltpu.CompilerParams(
            vmem_limit_bytes=DOTS_LIMIT if whole else VMEM_LIMIT
        ),
        cost_estimate=pl.CostEstimate(
            flops=rows * D, bytes_accessed=rows * D, transcendentals=0
        ),
    )(scalars, own_list, *dots, *bwd_terms, fwd_parts)


def final_kernel(width, *refs):
    taken, (best_ref, fwd_ref, bwd_ref) = refs[:-3], refs[-3:]
    total = taken[0][...]
    for ref in taken[1:]:
        total = total + ref[...]
    each, length = best_ref.shape
    rows = length // width
    fwd = total[each : each + 1] / (K * math.sqrt(D))
    fwd_ref[...] = fwd
    for v in range(width):
        part = total[each + 1 + v, 0:rows]
        bwd_ref[v * rows : (v + 1) * rows] = part.astype(jnp.bfloat16)
    best_ref[...] = total[:each] - 0.5 * fwd


def final_call(taken, width):
    length = taken[0].shape[1]
    vmem = pl.BlockSpec(memory_space=pltpu.VMEM)
    return pl.pallas_call(
        functools.partial(final_kernel, width),
        in_specs=[vmem] * len(taken),
        out_specs=[vmem] * 3,
        out_shape=[
            jax.ShapeDtypeStruct((CAND // width, length), jnp.float32),
            jax.ShapeDtypeStruct((1, length), jnp.float32),
            jax.ShapeDtypeStruct((length,), jnp.bfloat16),
        ],
        compiler_params=pltpu.CompilerParams(vmem_limit_bytes=16 * MIB),
    )(*taken)


def together(*values):
    return lax.optimization_barrier(values)


def on_device(source_vecs, target_vecs, fwd_owner, fwd_row, bwd_owner, bwd_row, cand_lists):
    reps = lax.axis_size("rep")
    planes = lax.axis_size("shard")
    width = lax.axis_size("width")
    shard = lax.axis_index("shard")
    wide = lax.axis_index("width")
    rep = lax.axis_index("rep")
    length = source_vecs.shape[0]
    rows = length // width
    parts = rows // BLOCK

    def part_of(values, index, axis=0):
        return lax.dynamic_slice_in_dim(values, index * rows, rows, axis)

    def shift(values, axis, count, by):
        return lax.ppermute(values, axis, [((i + by) % count, i) for i in range(count)])

    bidx = jnp.transpose(bwd_owner * length + bwd_row)
    codes = [bidx // CODE, lax.rem(bidx, CODE), jnp.zeros((EXTRA - 2 * K, length), jnp.int32)]
    codes = jnp.concatenate(codes).astype(jnp.bfloat16)
    first = [part_of(target_vecs, wide)]
    rest = []
    for d in range(1, width):
        index = lax.rem(wide + width - d, width)
        sent = part_of(target_vecs, index)
        if d == 1:
            sent = jnp.concatenate([sent, part_of(codes, index, 1)])
        rest.append(shift(sent, "width", width, d))
    fidx_own = jnp.transpose(fwd_owner * length + fwd_row)

    def over_reps(values):
        return jnp.stack([values] + [shift(values, "rep", reps, e) for e in range(1, reps)])

    fidx = over_reps(fidx_own)

    def moved(chunks, hop):
        out = []
        half = len(chunks) // 2
        ways = (chunks, chunks) if hop == 1 else (chunks[:half], chunks[half:])
        for by, side in zip((1, -1), ways):
            pairs = [(i, i + by) for i in range(planes) if 0 <= i + by < planes]
            pairs = [(i, j) for i, j in pairs if 0 <= j - by * hop < planes]
            out += [lax.ppermute(c, "shard", pairs) for c in side]
        return out

    both = (planes - 1) // 2
    queue = [(0, "own")]
    for hop in range(1, planes):
        queue += [(hop, "up"), (hop, "down")] if hop <= both else [(hop, "one")]
    dots, places, state, waiting = [], [], None, []
    scalars = jnp.stack([shard, wide, rep]).astype(jnp.int32)

    heads, tails = {0: first}, {0: rest}
    for hop in range(1, planes):
        heads[hop] = moved(heads[hop - 1], hop)
        if hop < 3:
            tails[hop] = moved(tails[hop - 1], hop)
    *_, fidx, held = together(*rest, fidx, source_vecs)
    sources = [held] + [shift(held, "width", width, d) for d in range(1, width)]
    got = together(*sources, *tails[1], *heads[2])
    sources = list(got[:width])
    src = [normalize_rows(sources)]
    for e in range(1, reps):
        src.append(shift(src[0], "rep", reps, e))

    def arrived(hop, side):
        half = len(tails[hop]) // 2
        return [heads[hop][side]] + tails[hop][side * half : side * half + half]

    for place, (hop, way) in enumerate(queue):
        if place == AHEAD:
            own_again, state[0] = together(fidx_own, state[0])
            fidx = over_reps(own_again)
            *late, fidx = together(*tails[2], fidx)
            tails[2] = list(late)
            for later in range(3, planes):
                tails[later] = moved(tails[later - 1], later)
        if way == "own":
            chunks = [first + rest]
        else:
            sides = {"up": (0,), "down": (1,), "one": (0, 1)}[way]
            chunks = [arrived(hop, side) for side in sides]
        waiting.append((hop, way, chunks))
        if place == 0 or place >= len(queue) - 2 or len(waiting) == 1:
            out, state = dots_call(scalars, fidx, src, waiting, state, planes)
            dots += out
            places += [(hop, way) for hop, way, _ in waiting]
            waiting = []

    def over_planes(values):
        if planes > 4:
            return [lax.psum(values, "shard")]
        return [values] + [shift(values, "shard", planes, d) for d in range(1, planes)]

    own_list = lax.dynamic_index_in_dim(cand_lists, shard, 0, keepdims=False)
    outs = margin_call(
        scalars, own_list, dots, over_planes(state[0]), state[1], tuple(places), width, planes <= 4
    )
    taken = [outs[0]]
    for d in range(1, width * reps):
        taken.append(shift(outs[d], ("width", "rep"), width * reps, d))
    best, fwd_mean, bwd_mean = final_call(taken, width)
    return (jnp.transpose(best), fwd_mean.reshape(-1), bwd_mean)


def solution(mesh):
    in_specs = (
        P(("groups", "shard", "rep"), "width"),
        P(("groups", "shard", "rep"), "width"),
        P(("groups", "shard", "rep"), None),
        P(("groups", "shard", "rep"), None),
        P(("groups", "shard", "rep"), None),
        P(("groups", "shard", "rep"), None),
        P("groups", None),
    )
    out_specs = (
        P(("groups", "shard", "rep"), "width"),
        P(("groups", "shard", "rep")),
        P(("groups", "shard", "rep")),
    )
    return jax.shard_map(
        on_device, mesh=mesh, in_specs=in_specs, out_specs=out_specs, check_vma=False
    )
```
